512 devices in a mesh: samp: 64 (over y, x, core), var: 8 (over z).
Axes of the slice: x: 4, y: 8, z: 8, core: 2. Of those that a mesh axis runs over, the one named last changes fastest.
Arguments:
- active_geno: bfloat16 [32768, 16384], P('samp', 'var'), may hold values from 0 to 2
- screen_geno: bfloat16 [32768, 16384], P('samp', 'var'), may hold values from 0 to 2
- beta: bfloat16 [16384, 32], P('var'), may hold values from -0.046875 to 0.046875
- counts: int32 [32, 32768], P(None, 'samp'), may hold values from 1 to 4
- ipcw: float32 [32768], P('samp'), may hold values from 1 to 5
- events: int32 [32768], P('samp'), may hold values 0 or 1
- order: int32 [64, 512], P('samp'), may hold values from 0 to 511, each once within a row
Outputs:
- grad_active: float32 [32, 16384], P(None, ('var', 'samp'))
- score_screen: float32 [32, 16384], P(None, ('var', 'samp'))
The draws below stay inside these ranges and needn't reach their ends.
Inputs may be any that keep to these rules, and one draw needn't show every extreme that they name: Each row of order holds every rank 0 to 511 once; blocks come in event-time order along samp.
All inputs are finite; a program needn't handle non-finite values. No bound on the sum of `events` on one device may be relied on, other than what follows from the above.
Results may differ from the reference program's by a relative error of at most 0.005.
Values sent between devices are 32-bit elements; how exact they have to be, the bound alone decides.
A program may use at most 64 MiB of HBM per device.

```python
import math
import jax
import jax.numpy as jnp
from jax import lax

PDEV = 512
ACT = 16384
SCR = 16384
BOOT = 32
NPART = 32768
BLOCKS = 64


def plant(array, stream_key, least, top_value):
    spot = [jax.random.randint(jax.random.fold_in(stream_key, axis), (), 0, length) for axis, length in enumerate(array.shape)]
    main_axis = array.shape.index(max(array.shape))
    beside = spot[:main_axis] + [(spot[main_axis] + 1) % array.shape[main_axis]] + spot[main_axis + 1:]
    return array.at[tuple(spot)].set(least).at[tuple(beside)].set(top_value)


def level_of(stream_key, shape, cuts, smallest, top_value):
    gain, own = 1.0, jax.random.fold_in(stream_key, 6)
    for dim, blocks in cuts:
        heights = jnp.exp(jax.random.uniform(jax.random.fold_in(own, dim), (blocks,), jnp.float32, smallest / len(cuts), top_value / len(cuts)))
        gain = gain * jnp.repeat(heights, shape[dim] // blocks).reshape([-1 if axis == dim else 1 for axis in range(len(shape))])
    return gain


def bell_draw(own_key, extent, scale, bound, cuts=(), kind=jnp.bfloat16):
    values = jax.random.normal(own_key, extent, jnp.float32) * scale
    if len(cuts) > 0:
        values = level_of(own_key, extent, cuts, -0.22, 0.18) * values
    return jnp.clip(values, min=-bound, max=bound).astype(kind)


def setup_inputs(seed: int = 0) -> dict:
    key_list = jax.random.split(jax.random.key(seed), 8)
    return {
        "active_geno": jnp.clip(2.0 * jax.random.uniform(key_list[0], (NPART, ACT), jnp.float32) ** level_of(key_list[0], (NPART, ACT), ((0, 64), (1, 8)), -0.2, 0.2), 0.0, 2.0).astype(jnp.bfloat16),
        "screen_geno": jnp.clip(2.0 * jax.random.uniform(key_list[1], (NPART, SCR), jnp.float32) ** level_of(key_list[1], (NPART, SCR), ((0, 64), (1, 8)), -0.2, 0.2), 0.0, 2.0).astype(jnp.bfloat16),
        "beta": bell_draw(key_list[2], (ACT, BOOT), ACT ** -0.5, 0.046875, ((0, 8),)),
        "counts": plant(jax.random.randint(key_list[3], (BOOT, NPART), 1, 5), jax.random.fold_in(key_list[3], 1), 1, 4).astype(jnp.int32),
        "ipcw": jnp.clip(jnp.exp(math.log(5.0) - 1.609438 * jax.random.uniform(key_list[4], (NPART,), jnp.float32) ** level_of(key_list[4], (NPART,), ((0, 64),), -0.2, 0.2)), 1.0, 5.0),
        "events": plant((jax.random.randint(key_list[5], (NPART,), 0, 2) < 1).astype(jnp.int32), jax.random.fold_in(key_list[5], 1), 0, 1),
        "order": jax.vmap(lambda own: jax.random.permutation(own, PDEV))(jax.random.split(key_list[6], BLOCKS)).reshape((BLOCKS, PDEV)).astype(jnp.int32),
    }


def reference(active_geno, screen_geno, beta, counts, ipcw, events, order):
    npart = active_geno.shape[0]
    wts = counts.astype(jnp.float32) * ipcw[None, :]
    eta = lax.dot_general(beta, active_geno, (((0,), (1,)), ((), ())), preferred_element_type=jnp.float32)
    risk = wts * jnp.exp(eta)
    blockwise = jnp.arange(BLOCKS, dtype=jnp.int32)[:, None] * PDEV + order.astype(jnp.int32)
    position = blockwise.reshape(-1).astype(jnp.int32)
    sorting = jnp.argsort(position).astype(jnp.int32)
    sorted_risk = risk[:, sorting]
    suffix = jnp.cumsum(sorted_risk[:, ::-1], axis=1)[:, ::-1]
    total_risk = suffix[:, position]
    flagged = events.astype(jnp.float32)[None, :] * wts
    haz = flagged / total_risk
    cum = jnp.cumsum(haz[:, sorting], axis=1)[:, position]
    resid = (flagged - risk * cum).astype(jnp.bfloat16)
    scale = float(npart) ** -0.5
    grad_active = lax.dot_general(resid, active_geno, (((1,), (0,)), ((), ())), preferred_element_type=jnp.float32) * scale
    score_screen = lax.dot_general(resid, screen_geno, (((1,), (0,)), ((), ())), preferred_element_type=jnp.float32) * scale
    return grad_active, score_screen
```

```python
import functools
import jax
import jax.numpy as jnp
from jax import lax
from jax.experimental import pallas as pl
from jax.experimental.pallas import tpu as pltpu
from jax.sharding import PartitionSpec as P

MESH = pl.DeviceIdType.MESH
NY, NX, NC, NZ = 8, 4, 2, 8
NG = NX * NC
HALF = 256
F32 = jnp.float32
BF16 = jnp.bfloat16


def lane_iota(shape):
    return lax.broadcasted_iota(jnp.int32, shape, 1)


def row_iota(shape):
    return lax.broadcasted_iota(jnp.int32, shape, 0)


def swap4(tile):
    return pltpu.roll(tile, 4, 0)


def fold_halves(low, high, upper):
    top = row_iota(low.shape) < 4
    even = jnp.where(top, low, swap4(high))
    odd = jnp.where(top, swap4(low), high)
    return jnp.where(upper, odd, even)


def split2(value):
    high = value.astype(BF16)
    rest = value - high.astype(F32)
    return jnp.concatenate([high.astype(F32), rest], axis=0).astype(BF16)


def masked_sums(value, mask_ref):
    pieces = split2(value)
    first = jnp.dot(pieces, mask_ref[0:HALF, :], preferred_element_type=F32)
    second = jnp.dot(pieces, mask_ref[HALF:, :], preferred_element_type=F32)
    first = first[0:8] + first[8:16]
    second = second[0:8] + second[8:16]
    top = row_iota((8, HALF)) < 4
    low = jnp.where(top, first[:, :HALF], second[:, :HALF])
    low = low + swap4(low)
    high = jnp.where(top, first[:, HALF:], second[:, HALF:])
    high = high + swap4(high)
    return jnp.where(top, low, high)


def to_lanes(value):
    total = jnp.sum(value, axis=1, keepdims=True)
    total = jnp.broadcast_to(total, (8, 128))
    total = total + swap4(total)
    lane, row = lane_iota((8, 128)), row_iota((8, 128))
    return jnp.sum(jnp.where(lane % 8 == row, total, 0.0), axis=0, keepdims=True)


def to_rows(value):
    lane, row = lane_iota((8, 128)), row_iota((8, 128))
    return jnp.sum(jnp.where(lane == row, jnp.broadcast_to(value, (8, 128)), 0.0), axis=1, keepdims=True)


def kernel(scale, active, screen, beta, counts, ipcw, events, order, grad, score,
           act_v, scr_v, beta_v, cnt_v, ipcw_v, ev_v, ord_v,
           later, earlier, eta_send, eta_recv, tot_send, tot_recv, res_send, res_all,
           core_send, core_recv, x_send, x_recv, y_send, y_recv,
           load_sem, eta_ss, eta_rs, tot_ss, tot_rs, res_ss, res_rs,
           core_ss, core_rs, x_ss, x_rs, y_ss, y_rs):
    s = lax.axis_index("samp")
    v = lax.axis_index("var")
    y, g = s // NG, s % NG
    x, c = g // NC, g % NC

    def zpeer(d):
        return (s, (v + d) % NZ)

    def gpeer(d):
        return (y * NG + (g + d) % NG, v)

    def ypeer(d):
        return (((y + d) % NY) * NG + g, v)

    def xpeer(d):
        return (y * NG + ((x + d) % NX) * NC + c, v)

    cpeer = (y * NG + x * NC + 1 - c, v)

    loads = [
        (order, ord_v), (beta, beta_v),
        (active.at[0:128], act_v.at[0:128]), (active.at[128:256], act_v.at[128:256]),
        (active.at[256:384], act_v.at[256:384]), (active.at[384:512], act_v.at[384:512]),
        (counts, cnt_v), (ipcw, ipcw_v), (events, ev_v), (screen, scr_v),
    ]
    loads = [pltpu.make_async_copy(a, b, load_sem.at[i]) for i, (a, b) in enumerate(loads)]
    for copy in loads:
        copy.start()

    barrier = pltpu.get_barrier_semaphore()
    for d in range(1, 8):
        for peer in (zpeer(d), gpeer(d), ypeer(d)):
            pl.semaphore_signal(barrier, inc=1, device_id=peer, device_id_type=MESH)

    def send(src, dst, ss, rs, peer):
        copy = pltpu.make_async_remote_copy(
            src_ref=src, dst_ref=dst, send_sem=ss, recv_sem=rs, device_id=peer, device_id_type=MESH)
        copy.start()
        return copy

    sent = []

    loads[0].wait()
    ranks = ord_v[...].astype(F32)
    for k in range(4):
        column = jnp.broadcast_to(ranks[:, k * 128:(k + 1) * 128], (128, 128)).T
        for j in range(4):
            line = jnp.broadcast_to(ranks[:, j * 128:(j + 1) * 128], (128, 128))
            later[k * 128:(k + 1) * 128, j * 128:(j + 1) * 128] = jnp.where(column >= line, 1.0, 0.0).astype(BF16)
            earlier[k * 128:(k + 1) * 128, j * 128:(j + 1) * 128] = jnp.where(column <= line, 1.0, 0.0).astype(BF16)

    loads[1].wait()
    coefs = beta_v[...]
    for k in range(4):
        loads[2 + k].wait()
        part = jnp.dot(act_v[k * 128:(k + 1) * 128, :], coefs, preferred_element_type=F32)
        part = part.T
        h, lanes = k // 2, slice((k % 2) * 128, (k % 2) * 128 + 128)
        for dest in range(NZ):
            eta_send[dest, 4 * h:4 * h + 4, lanes] = part[4 * dest:4 * dest + 4, :]
    pl.semaphore_wait(barrier, 21)
    for d in range(1, NZ):
        sent.append(send(eta_send.at[(v + d) % NZ], eta_recv.at[d - 1], eta_ss.at[d - 1], eta_rs.at[d - 1], zpeer(d)))
    etas = list(sent)

    for i in (6, 7, 8):
        loads[i].wait()
    tile = cnt_v[pl.ds(pl.multiple_of((v // 2) * 8, 8), 8), :].astype(F32)
    wts = fold_halves(tile[:, :HALF], tile[:, HALF:], v % 2 == 1)
    top = row_iota((8, HALF)) < 4

    def by_half(line):
        return jnp.where(top, jnp.broadcast_to(line[:, :HALF], (8, HALF)), jnp.broadcast_to(line[:, HALF:], (8, HALF)))

    wts = wts * by_half(ipcw_v[...])
    flagged = by_half(ev_v[...].astype(F32)) * wts

    eta = eta_send[v]
    for d in range(1, NZ):
        etas[d - 1].wait_recv()
        eta = eta + eta_recv[d - 1]
    risk = wts * jnp.exp(eta)

    def entering(total, n, reverse):
        base = 4 * n
        out = jnp.zeros((1, 128), F32)
        for step, (place, peer) in enumerate(((g, gpeer), (y, ypeer))):
            at = 2 * n + step
            tot_send[at] = total
            copies = []
            for d in range(1, 8):
                copies.append(send(tot_send.at[at], tot_recv.at[at, d - 1], tot_ss.at[at, d - 1], tot_rs.at[at, d - 1], peer(d)))
            sent.extend(copies)
            yield None
            for d in range(1, 8):
                copies[d - 1].wait_recv()
                got = tot_recv[at, d - 1]
                wanted = (d > place) if reverse else (d <= place)
                out = out + jnp.where(wanted, got, 0.0)
                total = total + got
        yield out

    walk = entering(to_lanes(risk), 0, True)
    next(walk)
    suffix = masked_sums(risk, later)
    next(walk)
    after = next(walk)
    haz = flagged / (suffix + to_rows(after))
    walk = entering(to_lanes(haz), 1, False)
    next(walk)
    prefix = masked_sums(haz, earlier)
    next(walk)
    before = next(walk)
    resid = flagged - risk * (prefix + to_rows(before))

    res_send[...] = resid
    copies = []
    for d in range(1, NZ):
        copies.append(send(res_send, res_all.at[v], res_ss.at[d - 1], res_rs.at[d - 1], zpeer(d)))
    sent.extend(copies)
    res_all[v] = resid
    for copy in copies:
        copy.wait_recv()
    lows, highs = [], []
    for u in range(4):
        one, two = res_all[2 * u], res_all[2 * u + 1]
        lows.append(jnp.where(top, one, swap4(two)))
        highs.append(jnp.where(top, swap4(one), two))
    low = jnp.concatenate(lows, axis=0).astype(BF16)
    high = jnp.concatenate(highs, axis=0).astype(BF16)
    lhs = jnp.concatenate([low, high], axis=1)

    loads[9].wait()
    lane = lane_iota((8, 128))
    first32 = (lane // 32) % 2 == 0
    first64 = lane < 64
    copies = []
    for k in range(NY):
        for a, geno in enumerate((act_v, scr_v)):
            block = jnp.dot(lhs, geno[:, k * 256:(k + 1) * 256], preferred_element_type=F32)
            for t in range(2):
                for p in range(2):
                    one = block[16 * p:16 * p + 8, t * 128:(t + 1) * 128]
                    two = block[16 * p + 8:16 * p + 16, t * 128:(t + 1) * 128]
                    core_send[0, k, a * 4 + t * 2 + p] = jnp.where(first32, one, pltpu.roll(two, 32, 1))
                    core_send[1, k, a * 4 + t * 2 + p] = jnp.where(first32, pltpu.roll(one, 96, 1), two)
        copies.append(send(core_send.at[1 - c, k], core_recv.at[k], core_ss.at[k], core_rs.at[k], cpeer))
    sent.extend(copies)
    for k in range(NY):
        copies[k].wait_recv()
        for a in range(2):
            for t in range(2):
                i = a * 4 + t * 2
                one = core_send[c, k, i] + core_recv[k, i]
                two = core_send[c, k, i + 1] + core_recv[k, i + 1]
                x_send[2 * t, k, a] = jnp.where(first64, one, pltpu.roll(two, 64, 1))
                x_send[2 * t + 1, k, a] = jnp.where(first64, pltpu.roll(one, 64, 1), two)
    copies = []
    for d in range(1, NX):
        copies.append(send(x_send.at[(x + d) % NX], x_recv.at[d - 1], x_ss.at[d - 1], x_rs.at[d - 1], xpeer(d)))
    sent.extend(copies)
    for copy in copies:
        copy.wait_recv()
    y_send[...] = x_send[x] + x_recv[0] + x_recv[1] + x_recv[2]
    copies = []
    for d in range(1, NY):
        copies.append(send(y_send.at[(y + d) % NY], y_recv.at[d - 1], y_ss.at[d - 1], y_rs.at[d - 1], ypeer(d)))
    sent.extend(copies)
    final = y_send[y]
    for d in range(1, NY):
        copies[d - 1].wait_recv()
        final = final + y_recv[d - 1]
    final = final * scale
    for a, out in enumerate((grad, score)):
        for q in range(4):
            turned = final[a] if q == 0 else pltpu.roll(final[a], 128 - 32 * q, 1)
            out[8 * q:8 * q + 8, :] = turned[:, :32]
    for copy in sent:
        copy.wait_send()


def per_device(active_geno, screen_geno, beta, counts, ipcw, events, order):
    rows, columns = active_geno.shape
    scale = float(rows * lax.axis_size("samp")) ** (-0.5)
    out = jax.ShapeDtypeStruct((32, 32), F32)
    dma = pltpu.SemaphoreType.DMA
    return pl.pallas_call(
        functools.partial(kernel, scale),
        out_shape=(out, out),
        in_specs=[pl.BlockSpec(memory_space=pl.ANY)] * 7,
        out_specs=[pl.BlockSpec(memory_space=pltpu.VMEM)] * 2,
        scratch_shapes=[
            pltpu.VMEM((rows, columns), BF16), pltpu.VMEM((rows, columns), BF16),
            pltpu.VMEM((columns, 32), BF16), pltpu.VMEM((32, rows), jnp.int32),
            pltpu.VMEM((1, rows), F32), pltpu.VMEM((1, rows), jnp.int32), pltpu.VMEM((1, rows), jnp.int32),
            pltpu.VMEM((rows, rows), BF16), pltpu.VMEM((rows, rows), BF16),
            pltpu.VMEM((NZ, 8, HALF), F32), pltpu.VMEM((NZ - 1, 8, HALF), F32),
            pltpu.VMEM((4, 1, 128), F32), pltpu.VMEM((4, 7, 1, 128), F32),
            pltpu.VMEM((8, HALF), F32), pltpu.VMEM((NZ, 8, HALF), F32),
            pltpu.VMEM((2, NY, 8, 8, 128), F32), pltpu.VMEM((NY, 8, 8, 128), F32),
            pltpu.VMEM((NX, NY, 2, 8, 128), F32), pltpu.VMEM((NX - 1, NY, 2, 8, 128), F32),
            pltpu.VMEM((NY, 2, 8, 128), F32), pltpu.VMEM((NY - 1, 2, 8, 128), F32),
            dma((10,)), dma((7,)), dma((7,)), dma((4, 7)), dma((4, 7)), dma((7,)), dma((7,)),
            dma((8,)), dma((8,)), dma((3,)), dma((3,)), dma((7,)), dma((7,)),
        ],
        compiler_params=pltpu.CompilerParams(
            collective_id=0, has_side_effects=True, vmem_limit_bytes=48 * 1024 * 1024),
    )(active_geno, screen_geno, beta, counts, ipcw.reshape(1, -1), events.reshape(1, -1), order)


def solution(mesh):
    placed = (
        P("samp", "var"),
        P("samp", "var"),
        P("var", None),
        P(None, "samp"),
        P("samp"),
        P("samp"),
        P("samp", None),
    )
    return jax.shard_map(
        per_device,
        mesh=mesh,
        in_specs=placed,
        out_specs=(P(None, ("var", "samp")), P(None, ("var", "samp"))),
        check_vma=False,
    )
```

```python
import functools
import jax
import jax.numpy as jnp
from jax import lax
from jax.experimental import pallas as pl
from jax.experimental.pallas import tpu as pltpu
from jax.sharding import PartitionSpec as P

MESH = pl.DeviceIdType.MESH
NY, NX, NC, NZ = 8, 4, 2, 8
CHIPS = NY * NX
BOOT = 32
HALF = 256
PARTS = 4
F32 = jnp.float32
BF16 = jnp.bfloat16


def ring(d, n):
    return min(d, n - d)


ZOFF = sorted(range(1, NZ), key=lambda d: -ring(d, NZ))
YOFF = sorted(range(NY), key=lambda d: -ring(d, NY))
XOFF = sorted(range(1, NX), key=lambda d: -ring(d, NX))
CHIPOFF = sorted(
    [(dy, dx) for dy in range(NY) for dx in range(NX) if dy or dx],
    key=lambda o: -(ring(o[0], NY) + ring(o[1], NX)))


def lane_iota(shape):
    return lax.broadcasted_iota(jnp.int32, shape, 1)


def row_iota(shape):
    return lax.broadcasted_iota(jnp.int32, shape, 0)


def swap4(tile):
    return pltpu.roll(tile, 4, 0)


def split2(value):
    high = value.astype(BF16)
    rest = (value - high.astype(F32)).astype(BF16)
    return jnp.concatenate([high, rest], axis=0)


def to_lanes(total):
    full = jnp.broadcast_to(total, (BOOT, 128))
    same = lane_iota((BOOT, 128)) == row_iota((BOOT, 128))
    return jnp.sum(jnp.where(same, full, 0.0), axis=0, keepdims=True)


def to_rows(line):
    full = jnp.broadcast_to(line, (BOOT, 128))
    same = lane_iota((BOOT, 128)) == row_iota((BOOT, 128))
    return jnp.sum(jnp.where(same, full, 0.0), axis=1, keepdims=True)


def kernel(scale, active, screen, beta, counts, ipcw, events, order, grad, score,
           act_v, scr_v, beta_v, cnt_v, ipcw_v, ev_v, ord_v,
           later, earlier, eta_send, eta_recv, sum_send, eta_all,
           tot_own, tot_peer, tot_chip, tot_recv,
           two_send, two_recv, core_send, core_recv, x_send, x_recv, y_send, y_recv,
           load_sem, eta_ss, eta_rs, all_ss, all_rs, pair_ss, pair_rs, chip_ss, chip_rs,
           two_ss, two_rs, core_ss, core_rs, x_ss, x_rs, y_ss, y_rs):
    s = lax.axis_index("samp")
    v = lax.axis_index("var")
    y, g = s // (NX * NC), s % (NX * NC)
    x, c = g // NC, g % NC
    ybase = [((y + d) % NY) * (NX * NC) for d in range(NY)]
    xbase = [((x + d) % NX) * NC + c for d in range(NX)]
    chip = y * NX + x

    def zpeer(d):
        return (s, (v + d) % NZ)

    def chippeer(dy, dx):
        return (ybase[dy] + xbase[dx], v)

    cpeer = (y * (NX * NC) + x * NC + 1 - c, v)

    loads = [
        (order, ord_v), (beta, beta_v),
        (active.at[0:128], act_v.at[0:128]), (active.at[128:256], act_v.at[128:256]),
        (active.at[256:384], act_v.at[256:384]), (active.at[384:512], act_v.at[384:512]),
        (counts, cnt_v), (ipcw, ipcw_v), (events, ev_v), (screen, scr_v),
    ]
    loads = [pltpu.make_async_copy(a, b, load_sem.at[i]) for i, (a, b) in enumerate(loads)]
    for copy in loads:
        copy.start()

    barrier = pltpu.get_barrier_semaphore()

    def greet(peer):
        pl.semaphore_signal(barrier, inc=1, device_id=peer, device_id_type=MESH)

    for d in ZOFF:
        greet(zpeer(d))
    for dy, dx in CHIPOFF:
        greet(chippeer(dy, dx))
    greet(cpeer)

    def send(src, dst, ss, rs, peer):
        pltpu.make_async_remote_copy(
            src_ref=src, dst_ref=dst, send_sem=ss, recv_sem=rs, device_id=peer, device_id_type=MESH).start()

    def await_bytes(ref, sem):
        pltpu.make_async_copy(ref, ref, sem).wait()

    loads[1].wait()
    coefs = beta_v[...]
    for k in range(4):
        loads[2 + k].wait()
        part = lax.dot_general(
            coefs, act_v[k * 128:(k + 1) * 128, :], (((1,), (1,)), ((), ())), preferred_element_type=F32)
        h, lanes = k // 2, slice((k % 2) * 128, (k % 2) * 128 + 128)
        for dest in range(NZ):
            eta_send[dest, 4 * h:4 * h + 4, lanes] = part[4 * dest:4 * dest + 4, :]
    pl.semaphore_wait(barrier, NZ - 1 + CHIPS - 1 + 1)
    for d in ZOFF:
        send(eta_send.at[(v + d) % NZ], eta_recv.at[d - 1], eta_ss, eta_rs, zpeer(d))

    loads[0].wait()
    ranks = ord_v[...].astype(F32)
    for k in range(4):
        column = jnp.broadcast_to(ranks[:, k * 128:(k + 1) * 128], (128, 128)).T
        for j in range(4):
            line = jnp.broadcast_to(ranks[:, j * 128:(j + 1) * 128], (128, 128))
            later[k * 128:(k + 1) * 128, j * 128:(j + 1) * 128] = jnp.where(column >= line, 1.0, 0.0).astype(BF16)
            earlier[k * 128:(k + 1) * 128, j * 128:(j + 1) * 128] = jnp.where(column <= line, 1.0, 0.0).astype(BF16)
    for i in (6, 7, 8):
        loads[i].wait()
    wts = cnt_v[...].astype(F32) * ipcw_v[...]
    flagged = ev_v[...].astype(F32) * wts

    await_bytes(eta_recv, eta_rs)
    eta = eta_send[v]
    for d in range(1, NZ):
        eta = eta + eta_recv[d - 1]
    sum_send[...] = eta
    for d in ZOFF:
        send(sum_send, eta_all.at[v], all_ss, all_rs, zpeer(d))
    eta_all[v] = eta
    await_bytes(eta_all.at[0:NZ - 1], all_rs)
    top = row_iota((8, HALF)) < 4
    lows, highs = [], []
    for u in range(4):
        one, two = eta_all[2 * u], eta_all[2 * u + 1]
        lows.append(jnp.where(top, one, swap4(two)))
        highs.append(jnp.where(top, swap4(one), two))
    eta = jnp.concatenate([jnp.concatenate(lows, axis=0), jnp.concatenate(highs, axis=0)], axis=1)
    risk = wts * jnp.exp(eta)

    def pair_start(n, total):
        tot_own[n] = total
        send(tot_own.at[n], tot_peer.at[n], pair_ss.at[n], pair_rs.at[n], cpeer)

    def chip_start(n, total):
        await_bytes(tot_peer.at[n], pair_rs.at[n])
        peer = tot_peer[n]
        tot_chip[n] = total + peer
        for dy, dx in CHIPOFF:
            send(tot_chip.at[n], tot_recv.at[n, chip], chip_ss.at[n], chip_rs.at[n], chippeer(dy, dx))
        return peer

    def chip_end(n, wanted):
        await_bytes(tot_recv.at[n, 0:CHIPS - 1], chip_rs.at[n])
        out = jnp.zeros((1, 128), F32)
        for k in range(CHIPS):
            out = out + jnp.where(wanted(k), tot_recv[n, k], 0.0)
        return out

    lane = lane_iota((8, 128))
    first32 = (lane // 32) % 2 == 0
    first64 = lane < 64

    def project(pieces, j, out):
        place = pl.multiple_of(((y + YOFF[j]) % NY) * HALF, HALF)
        for a, geno in enumerate((act_v, scr_v)):
            block = jnp.dot(pieces, geno[:, pl.ds(place, HALF)], preferred_element_type=F32)
            block = block[:BOOT] + block[BOOT:]
            for t in range(2):
                for p in range(2):
                    one = block[16 * p:16 * p + 8, t * 128:(t + 1) * 128]
                    two = block[16 * p + 8:16 * p + 16, t * 128:(t + 1) * 128]
                    out[0, j, a * 4 + t * 2 + p] = jnp.where(first32, one, pltpu.roll(two, 32, 1))
                    out[1, j, a * 4 + t * 2 + p] = jnp.where(first32, pltpu.roll(one, 96, 1), two)

    total = to_lanes(jnp.sum(risk, axis=1, keepdims=True))
    pair_start(0, total)
    pieces = split2(risk)
    suffix = jnp.dot(pieces, later[...], preferred_element_type=F32)
    suffix = suffix[:BOOT] + suffix[BOOT:]
    peer = chip_start(0, total)
    loads[9].wait()
    for j in range(NY):
        project(pieces, j, two_send)
    send(two_send.at[1 - c], two_recv, two_ss, two_rs, cpeer)
    after = chip_end(0, lambda k: k > chip)
    after = after + jnp.where(c == 0, peer, 0.0)
    haz = flagged / (suffix + to_rows(after))

    total = to_lanes(jnp.sum(haz, axis=1, keepdims=True))
    pair_start(1, total)
    prefix = jnp.dot(split2(haz), earlier[...], preferred_element_type=F32)
    prefix = prefix[:BOOT] + prefix[BOOT:]
    peer = chip_start(1, total)
    pieces = split2(flagged - risk * prefix)
    for j in range(NY):
        project(pieces, j, core_send)
        send(core_send.at[1 - c, j], core_recv.at[j], core_ss.at[j], core_rs.at[j], cpeer)
    await_bytes(two_recv, two_rs)
    before = chip_end(1, lambda k: k < chip)

    def factors(line):
        rows = jnp.broadcast_to(to_rows(line), (BOOT, 128))
        return [jnp.where(first32, rows[16 * p:16 * p + 8], rows[16 * p + 8:16 * p + 16]) for p in range(2)]

    mine = factors(before + jnp.where(c == 1, peer, 0.0))
    other = factors(before + jnp.where(c == 0, total, 0.0))

    size = NY // PARTS
    for part in range(PARTS):
        for j in range(part * size, (part + 1) * size):
            await_bytes(core_recv.at[j], core_rs.at[j])
            for a in range(2):
                for t in range(2):
                    both = []
                    for p in range(2):
                        i = a * 4 + t * 2 + p
                        both.append(
                            core_send[c, j, i] + core_recv[j, i]
                            - (mine[p] * two_send[c, j, i] + other[p] * two_recv[j, i]))
                    one, two = both
                    x_send[2 * t, j, a] = jnp.where(first64, one, pltpu.roll(two, 64, 1))
                    x_send[2 * t + 1, j, a] = jnp.where(first64, pltpu.roll(one, 64, 1), two)
        piece = pl.ds(part * size, size)
        for d in XOFF:
            send(x_send.at[(x + d) % NX, piece], x_recv.at[part, d - 1], x_ss, x_rs.at[part], chippeer(0, d))
    for part in range(PARTS):
        await_bytes(x_recv.at[part], x_rs.at[part])
        for j in range(part * size, (part + 1) * size):
            i = j - part * size
            y_send[j] = (x_send[x, j] + x_recv[part, 0, i]) + (x_recv[part, 1, i] + x_recv[part, 2, i])
            if YOFF[j]:
                send(y_send.at[j], y_recv.at[j], y_ss, y_rs, chippeer(YOFF[j], 0))
    await_bytes(eta_recv, eta_ss)
    await_bytes(eta_all.at[0:NZ - 1], all_ss)
    for n in range(2):
        await_bytes(tot_peer.at[n], pair_ss.at[n])
        await_bytes(tot_recv.at[n, 0:CHIPS - 1], chip_ss.at[n])
    await_bytes(two_recv, two_ss)
    for j in range(NY):
        await_bytes(core_recv.at[j], core_ss.at[j])
    await_bytes(x_recv, x_ss)
    await_bytes(y_recv, y_rs)
    final = y_send[NY - 1]
    for j in range(NY - 1):
        final = final + y_recv[j]
    final = final * scale
    for a, out in enumerate((grad, score)):
        for q in range(4):
            turned = final[a] if q == 0 else pltpu.roll(final[a], 128 - 32 * q, 1)
            out[8 * q:8 * q + 8, :] = turned[:, :32]
    await_bytes(y_recv, y_ss)


def per_device(active_geno, screen_geno, beta, counts, ipcw, events, order):
    rows, columns = active_geno.shape
    scale = float(rows * lax.axis_size("samp")) ** (-0.5)
    out = jax.ShapeDtypeStruct((32, 32), F32)
    dma = pltpu.SemaphoreType.DMA
    return pl.pallas_call(
        functools.partial(kernel, scale),
        out_shape=(out, out),
        in_specs=[pl.BlockSpec(memory_space=pltpu.HBM)] * 7,
        out_specs=[pl.BlockSpec(memory_space=pltpu.VMEM)] * 2,
        scratch_shapes=[
            pltpu.VMEM((rows, columns), BF16), pltpu.VMEM((rows, columns), BF16),
            pltpu.VMEM((32, columns), BF16), pltpu.VMEM((32, rows), jnp.int32),
            pltpu.VMEM((1, rows), F32), pltpu.VMEM((1, rows), jnp.int32), pltpu.VMEM((1, rows), jnp.int32),
            pltpu.VMEM((rows, rows), BF16), pltpu.VMEM((rows, rows), BF16),
            pltpu.VMEM((NZ, 8, HALF), F32), pltpu.VMEM((NZ - 1, 8, HALF), F32),
            pltpu.VMEM((8, HALF), F32), pltpu.VMEM((NZ, 8, HALF), F32),
            pltpu.VMEM((2, 1, 128), F32), pltpu.VMEM((2, 1, 128), F32),
            pltpu.VMEM((2, 1, 128), F32), pltpu.VMEM((2, CHIPS, 1, 128), F32),
            pltpu.VMEM((2, NY, 8, 8, 128), F32), pltpu.VMEM((NY, 8, 8, 128), F32),
            pltpu.VMEM((2, NY, 8, 8, 128), F32), pltpu.VMEM((NY, 8, 8, 128), F32),
            pltpu.VMEM((NX, NY, 2, 8, 128), F32), pltpu.VMEM((PARTS, NX - 1, NY // PARTS, 2, 8, 128), F32),
            pltpu.VMEM((NY, 2, 8, 128), F32), pltpu.VMEM((NY - 1, 2, 8, 128), F32),
            dma((10,)), dma, dma, dma, dma, dma((2,)), dma((2,)), dma((2,)), dma((2,)),
            dma, dma, dma((NY,)), dma((NY,)), dma, dma((PARTS,)), dma, dma,
        ],
        compiler_params=pltpu.CompilerParams(
            collective_id=0, has_side_effects=True, vmem_limit_bytes=60 * 1024 * 1024),
    )(active_geno, screen_geno, beta.T, counts, ipcw.reshape(1, -1), events.reshape(1, -1), order)


def solution(mesh):
    placed = (
        P("samp", "var"),
        P("samp", "var"),
        P("var", None),
        P(None, "samp"),
        P("samp"),
        P("samp"),
        P("samp", None),
    )
    return jax.shard_map(
        per_device,
        mesh=mesh,
        in_specs=placed,
        out_specs=(P(None, ("var", "samp")), P(None, ("var", "samp"))),
        check_vma=False,
    )
```

```python
import functools
import jax
import jax.numpy as jnp
from jax import lax
from jax.experimental import pallas as pl
from jax.experimental.pallas import tpu as pltpu
from jax.sharding import PartitionSpec as P

MESH = pl.DeviceIdType.MESH
NY, NX, NC, NZ = 8, 4, 2, 8
CHIPS = NY * NX
BOOT = 32
HALF = 256
PARTS = 4
LAG = 3
F32 = jnp.float32
BF16 = jnp.bfloat16


def ring(d, n):
    return min(d, n - d)


ZOFF = sorted(range(1, NZ), key=lambda d: -ring(d, NZ))
YOFF = sorted(range(NY), key=lambda d: -ring(d, NY))
XOFF = sorted(range(1, NX), key=lambda d: -ring(d, NX))
CHIPOFF = sorted(
    [(dy, dx) for dy in range(NY) for dx in range(NX) if dy or dx],
    key=lambda o: -(ring(o[0], NY) + ring(o[1], NX)))


def lane_iota(shape):
    return lax.broadcasted_iota(jnp.int32, shape, 1)


def row_iota(shape):
    return lax.broadcasted_iota(jnp.int32, shape, 0)


def swap4(tile):
    return pltpu.roll(tile, 4, 0)


def split2(value):
    high = value.astype(BF16)
    rest = (value - high.astype(F32)).astype(BF16)
    return jnp.concatenate([high, rest], axis=0)


def to_lanes(total):
    full = jnp.broadcast_to(total, (BOOT, 128))
    same = lane_iota((BOOT, 128)) == row_iota((BOOT, 128))
    return jnp.sum(jnp.where(same, full, 0.0), axis=0, keepdims=True)


def to_rows(line):
    full = jnp.broadcast_to(line, (BOOT, 128))
    same = lane_iota((BOOT, 128)) == row_iota((BOOT, 128))
    return jnp.sum(jnp.where(same, full, 0.0), axis=1, keepdims=True)


def kernel(scale, active, screen, beta, counts, ipcw, events, order, result,
           act_v, scr_v, beta_v, cnt_v, ipcw_v, ev_v, ord_v,
           later, earlier, eta_send, eta_recv, sum_send, eta_all,
           tot_own, tot_peer, tot_chip, tot_recv,
           two_send, two_recv, core_send, core_recv, far_send, far_recv, x_send, x_recv, y_send, y_recv,
           load_sem, eta_ss, eta_rs, all_ss, all_rs, pair_ss, pair_rs, chip_ss, chip_rs,
           two_ss, two_rs, core_ss, core_rs, far_ss, far_rs, x_ss, x_rs, y_ss, y_rs):
    s = lax.axis_index("samp")
    v = lax.axis_index("var")
    y, g = s // (NX * NC), s % (NX * NC)
    x, c = g // NC, g % NC
    ybase = [((y + d) % NY) * (NX * NC) for d in range(NY)]
    xbase = [((x + d) % NX) * NC + c for d in range(NX)]
    chip = y * NX + x

    def zpeer(d):
        return (s, (v + d) % NZ)

    def chippeer(dy, dx):
        return (ybase[dy] + xbase[dx], v)

    cpeer = (y * (NX * NC) + x * NC + 1 - c, v)

    loads = [
        (order, ord_v), (beta, beta_v),
        (active.at[0:128], act_v.at[0:128]), (active.at[128:256], act_v.at[128:256]),
        (active.at[256:384], act_v.at[256:384]), (active.at[384:512], act_v.at[384:512]),
        (counts, cnt_v), (ipcw, ipcw_v), (events, ev_v), (screen, scr_v),
    ]
    loads = [pltpu.make_async_copy(a, b, load_sem.at[i]) for i, (a, b) in enumerate(loads)]
    for copy in loads:
        copy.start()

    barrier = pltpu.get_barrier_semaphore()

    def greet(peer):
        pl.semaphore_signal(barrier, inc=1, device_id=peer, device_id_type=MESH)

    for d in ZOFF:
        greet(zpeer(d))
    for dy, dx in CHIPOFF:
        greet(chippeer(dy, dx))
    greet(cpeer)

    def send(src, dst, ss, rs, peer):
        pltpu.make_async_remote_copy(
            src_ref=src, dst_ref=dst, send_sem=ss, recv_sem=rs, device_id=peer, device_id_type=MESH).start()

    def await_bytes(ref, sem):
        pltpu.make_async_copy(ref, ref, sem).wait()

    loads[1].wait()
    coefs = beta_v[...]
    for k in range(4):
        loads[2 + k].wait()
        part = lax.dot_general(
            coefs, act_v[k * 128:(k + 1) * 128, :], (((1,), (1,)), ((), ())), preferred_element_type=F32)
        h, lanes = k // 2, slice((k % 2) * 128, (k % 2) * 128 + 128)
        for dest in range(NZ):
            eta_send[dest, 4 * h:4 * h + 4, lanes] = part[4 * dest:4 * dest + 4, :]
    pl.semaphore_wait(barrier, NZ - 1 + CHIPS - 1 + 1)
    for d in ZOFF:
        send(eta_send.at[(v + d) % NZ], eta_recv.at[d - 1], eta_ss, eta_rs, zpeer(d))

    loads[0].wait()
    ranks = ord_v[...].astype(F32)
    for k in range(4):
        column = jnp.broadcast_to(ranks[:, k * 128:(k + 1) * 128], (128, 128)).T
        for j in range(4):
            line = jnp.broadcast_to(ranks[:, j * 128:(j + 1) * 128], (128, 128))
            later[k * 128:(k + 1) * 128, j * 128:(j + 1) * 128] = jnp.where(column >= line, 1.0, 0.0).astype(BF16)
            earlier[k * 128:(k + 1) * 128, j * 128:(j + 1) * 128] = jnp.where(column <= line, 1.0, 0.0).astype(BF16)
    for i in (6, 7, 8):
        loads[i].wait()
    wts = cnt_v[...].astype(F32) * ipcw_v[...]
    flagged = ev_v[...].astype(F32) * wts

    await_bytes(eta_recv, eta_rs)
    eta = eta_send[v]
    for d in range(1, NZ):
        eta = eta + eta_recv[d - 1]
    sum_send[...] = eta
    for d in ZOFF:
        send(sum_send, eta_all.at[v], all_ss, all_rs, zpeer(d))
    eta_all[v] = eta
    await_bytes(eta_all.at[0:NZ - 1], all_rs)
    top = row_iota((8, HALF)) < 4
    lows, highs = [], []
    for u in range(4):
        one, two = eta_all[2 * u], eta_all[2 * u + 1]
        lows.append(jnp.where(top, one, swap4(two)))
        highs.append(jnp.where(top, swap4(one), two))
    eta = jnp.concatenate([jnp.concatenate(lows, axis=0), jnp.concatenate(highs, axis=0)], axis=1)
    risk = wts * jnp.exp(eta)

    def pair_start(n, total):
        tot_own[n] = total
        send(tot_own.at[n], tot_peer.at[n], pair_ss.at[n], pair_rs.at[n], cpeer)

    def pair_end(n, total):
        await_bytes(tot_peer.at[n], pair_rs.at[n])
        peer = tot_peer[n]
        tot_chip[n] = total + peer
        return peer

    def chip_send(n, offsets):
        for dy, dx in offsets:
            send(tot_chip.at[n], tot_recv.at[n, chip], chip_ss.at[n], chip_rs.at[n], chippeer(dy, dx))

    def chip_end(n, wanted):
        await_bytes(tot_recv.at[n, 0:CHIPS - 1], chip_rs.at[n])
        out = jnp.zeros((1, 128), F32)
        for k in range(CHIPS):
            out = out + jnp.where(wanted(k), tot_recv[n, k], 0.0)
        return out

    lane = lane_iota((8, 128))
    first32 = (lane // 32) % 2 == 0
    first64 = lane < 64

    def project(pieces, j, out):
        place = pl.multiple_of(((y + YOFF[j]) % NY) * HALF, HALF)
        for a, geno in enumerate((act_v, scr_v)):
            block = jnp.dot(pieces, geno[:, pl.ds(place, HALF)], preferred_element_type=F32)
            block = block[:BOOT] + block[BOOT:]
            for t in range(2):
                for p in range(2):
                    one = block[16 * p:16 * p + 8, t * 128:(t + 1) * 128]
                    two = block[16 * p + 8:16 * p + 16, t * 128:(t + 1) * 128]
                    out[0, j, a * 4 + t * 2 + p] = jnp.where(first32, one, pltpu.roll(two, 32, 1))
                    out[1, j, a * 4 + t * 2 + p] = jnp.where(first32, pltpu.roll(one, 96, 1), two)

    def spread(mine, theirs, j, out):
        for a in range(2):
            for t in range(2):
                i = a * 4 + t * 2
                one = mine[c, j, i] + theirs[j, i]
                two = mine[c, j, i + 1] + theirs[j, i + 1]
                out[2 * t, j, a] = jnp.where(first64, one, pltpu.roll(two, 64, 1))
                out[2 * t + 1, j, a] = jnp.where(first64, pltpu.roll(one, 64, 1), two)

    total = to_lanes(jnp.sum(risk, axis=1, keepdims=True))
    pair_start(0, total)
    pieces = split2(risk)
    peer = pair_end(0, total)
    chip_send(0, CHIPOFF)
    suffix = jnp.dot(pieces, later[...], preferred_element_type=F32)
    suffix = suffix[:BOOT] + suffix[BOOT:]
    loads[9].wait()
    for j in range(NY):
        project(pieces, j, two_send)
    send(two_send.at[1 - c], two_recv, two_ss, two_rs, cpeer)
    await_bytes(two_recv, two_rs)
    for j in range(NY):
        spread(two_send, two_recv, j, far_send)
    for d in XOFF:
        send(far_send.at[(x + d) % NX], far_recv.at[d - 1], far_ss, far_rs, chippeer(0, d))

    after = chip_end(0, lambda k: k > chip)
    after = after + jnp.where(c == 0, peer, 0.0)
    haz = flagged / (suffix + to_rows(after))

    total = to_lanes(jnp.sum(haz, axis=1, keepdims=True))
    pair_start(1, total)
    prefix = jnp.dot(split2(haz), earlier[...], preferred_element_type=F32)
    prefix = prefix[:BOOT] + prefix[BOOT:]
    peer = pair_end(1, total)
    prefix = prefix + to_rows(jnp.where(c == 1, peer, 0.0))
    pieces = split2(flagged - risk * prefix)

    size = NY // PARTS

    def to_x(j):
        await_bytes(core_recv.at[j], core_rs.at[j])
        spread(core_send, core_recv, j, x_send)
        if (j + 1) % size == 0:
            part = j // size
            piece = pl.ds(part * size, size)
            for d in XOFF:
                send(x_send.at[(x + d) % NX, piece], x_recv.at[part, d - 1], x_ss, x_rs.at[part], chippeer(0, d))

    for j in range(NY):
        project(pieces, j, core_send)
        send(core_send.at[1 - c, j], core_recv.at[j], core_ss.at[j], core_rs.at[j], cpeer)
        chip_send(1, CHIPOFF[4 * j:4 * j + 4])
        if j >= LAG:
            to_x(j - LAG)
    for j in range(NY - LAG, NY):
        to_x(j)

    line = chip_end(1, lambda k: k < NX * y)
    ahead = []
    for k in range(NX):
        ahead.append(line)
        line = line + jnp.where(x == k, tot_chip[1], tot_recv[1, NX * y + k])
    factors = []
    for d in range(NX):
        at = (x - d + NX) % NX
        line = ahead[0]
        for k in range(1, NX):
            line = jnp.where(at == k, ahead[k], line)
        rows = jnp.broadcast_to(to_rows(line), (BOOT, 128))
        tile = rows[0:8]
        for q in range(1, 4):
            tile = jnp.where(lane // 32 == q, rows[8 * q:8 * q + 8], tile)
        factors.append(tile)
    await_bytes(far_recv, far_rs)
    for part in range(PARTS):
        await_bytes(x_recv.at[part], x_rs.at[part])
        for j in range(part * size, (part + 1) * size):
            i = j - part * size
            less = factors[0] * far_send[x, j] + factors[1] * far_recv[0, j]
            less = less + (factors[2] * far_recv[1, j] + factors[3] * far_recv[2, j])
            full = (x_send[x, j] + x_recv[part, 0, i]) + (x_recv[part, 1, i] + x_recv[part, 2, i])
            y_send[j] = full - less
            if YOFF[j]:
                send(y_send.at[j], y_recv.at[j], y_ss, y_rs, chippeer(YOFF[j], 0))
    await_bytes(eta_recv, eta_ss)
    await_bytes(eta_all.at[0:NZ - 1], all_ss)
    for n in range(2):
        await_bytes(tot_peer.at[n], pair_ss.at[n])
        await_bytes(tot_recv.at[n, 0:CHIPS - 1], chip_ss.at[n])
    await_bytes(two_recv, two_ss)
    for j in range(NY):
        await_bytes(core_recv.at[j], core_ss.at[j])
    await_bytes(x_recv, x_ss)
    await_bytes(far_recv, far_ss)
    await_bytes(y_recv, y_rs)
    final = y_send[NY - 1]
    for j in range(NY - 1):
        final = final + y_recv[j]
    final = final * scale
    for a in range(2):
        for q in range(4):
            turned = final[a] if q == 0 else pltpu.roll(final[a], 128 - 32 * q, 1)
            result[a, 8 * q:8 * q + 8, :] = turned[:, :32]
    await_bytes(y_recv, y_ss)


def per_device(active_geno, screen_geno, beta, counts, ipcw, events, order):
    rows, columns = active_geno.shape
    scale = float(rows * lax.axis_size("samp")) ** (-0.5)
    out = jax.ShapeDtypeStruct((2, BOOT, 32), F32)
    dma = pltpu.SemaphoreType.DMA
    result = pl.pallas_call(
        functools.partial(kernel, scale),
        out_shape=out,
        in_specs=[pl.BlockSpec(memory_space=pltpu.HBM)] * 7,
        out_specs=pl.BlockSpec(memory_space=pltpu.VMEM),
        scratch_shapes=[
            pltpu.VMEM((rows, columns), BF16), pltpu.VMEM((rows, columns), BF16),
            pltpu.VMEM((32, columns), BF16), pltpu.VMEM((32, rows), jnp.int32),
            pltpu.VMEM((1, rows), F32), pltpu.VMEM((1, rows), jnp.int32), pltpu.VMEM((1, rows), jnp.int32),
            pltpu.VMEM((rows, rows), BF16), pltpu.VMEM((rows, rows), BF16),
            pltpu.VMEM((NZ, 8, HALF), F32), pltpu.VMEM((NZ - 1, 8, HALF), F32),
            pltpu.VMEM((8, HALF), F32), pltpu.VMEM((NZ, 8, HALF), F32),
            pltpu.VMEM((2, 1, 128), F32), pltpu.VMEM((2, 1, 128), F32),
            pltpu.VMEM((2, 1, 128), F32), pltpu.VMEM((2, CHIPS, 1, 128), F32),
            pltpu.VMEM((2, NY, 8, 8, 128), F32), pltpu.VMEM((NY, 8, 8, 128), F32),
            pltpu.VMEM((2, NY, 8, 8, 128), F32), pltpu.VMEM((NY, 8, 8, 128), F32),
            pltpu.VMEM((NX, NY, 2, 8, 128), F32), pltpu.VMEM((NX - 1, NY, 2, 8, 128), F32),
            pltpu.VMEM((NX, NY, 2, 8, 128), F32), pltpu.VMEM((PARTS, NX - 1, NY // PARTS, 2, 8, 128), F32),
            pltpu.VMEM((NY, 2, 8, 128), F32), pltpu.VMEM((NY - 1, 2, 8, 128), F32),
            dma((10,)), dma, dma, dma, dma, dma((2,)), dma((2,)), dma((2,)), dma((2,)),
            dma, dma, dma((NY,)), dma((NY,)), dma, dma, dma, dma((PARTS,)), dma, dma,
        ],
        compiler_params=pltpu.CompilerParams(
            collective_id=0, has_side_effects=True, vmem_limit_bytes=60 * 1024 * 1024),
    )(active_geno, screen_geno, beta.T, counts, ipcw.reshape(1, -1), events.reshape(1, -1), order)
    return result[0], result[1]


def solution(mesh):
    placed = (
        P("samp", "var"),
        P("samp", "var"),
        P("var", None),
        P(None, "samp"),
        P("samp"),
        P("samp"),
        P("samp", None),
    )
    return jax.shard_map(
        per_device,
        mesh=mesh,
        in_specs=placed,
        out_specs=(P(None, ("var", "samp")), P(None, ("var", "samp"))),
        check_vma=False,
    )
```

```python
import functools
import jax
import jax.numpy as jnp
from jax import lax
from jax.experimental import pallas as pl
from jax.experimental.pallas import tpu as pltpu
from jax.sharding import PartitionSpec as P

MESH = pl.DeviceIdType.MESH
NY, NX, NC, NZ = 8, 4, 2, 8
CHIPS = NY * NX
BOOT = 32
HALF = 256
PARTS = 4
LAG = 3
F32 = jnp.float32
BF16 = jnp.bfloat16


def ring(d, n):
    return min(d, n - d)


ZOFF = sorted(range(1, NZ), key=lambda d: -ring(d, NZ))
YOFF = sorted(range(NY), key=lambda d: -ring(d, NY))
XOFF = sorted(range(1, NX), key=lambda d: -ring(d, NX))
CHIPOFF = sorted(
    [(dy, dx) for dy in range(NY) for dx in range(NX) if dy or dx],
    key=lambda o: -(ring(o[0], NY) + ring(o[1], NX)))


def lane_iota(shape):
    return lax.broadcasted_iota(jnp.int32, shape, 1)


def row_iota(shape):
    return lax.broadcasted_iota(jnp.int32, shape, 0)


def swap4(tile):
    return pltpu.roll(tile, 4, 0)


def split2(value):
    high = value.astype(BF16)
    rest = (value - high.astype(F32)).astype(BF16)
    return jnp.concatenate([high, rest], axis=0)


def to_lanes(total):
    full = jnp.broadcast_to(total, (BOOT, 128))
    same = lane_iota((BOOT, 128)) == row_iota((BOOT, 128))
    return jnp.sum(jnp.where(same, full, 0.0), axis=0, keepdims=True)


def to_rows(line):
    full = jnp.broadcast_to(line, (BOOT, 128))
    same = lane_iota((BOOT, 128)) == row_iota((BOOT, 128))
    return jnp.sum(jnp.where(same, full, 0.0), axis=1, keepdims=True)


def kernel(scale, active, screen, beta, counts, ipcw, events, order, result,
           act_v, scr_v, beta_v, cnt_v, ipcw_v, ev_v, ord_v,
           later, earlier, eta_send, eta_recv, sum_send, eta_all,
           risk_own, risk_all, tot_own, tot_peer, tot_chip, tot_recv,
           two_send, two_recv, core_send, core_recv, far_send, far_recv, x_send, x_recv, y_send, y_recv,
           load_sem, eta_ss, eta_rs, all_ss, all_rs, risk_ss, risk_rs, pair_ss, pair_rs, chip_ss, chip_rs,
           two_ss, two_rs, core_ss, core_rs, far_ss, far_rs, x_ss, x_rs, y_ss, y_rs, ready):
    s = lax.axis_index("samp")
    v = lax.axis_index("var")
    y, g = s // (NX * NC), s % (NX * NC)
    x, c = g // NC, g % NC
    ybase = [((y + d) % NY) * (NX * NC) for d in range(NY)]
    xbase = [((x + d) % NX) * NC + c for d in range(NX)]
    chip = y * NX + x

    def zpeer(d):
        return (s, (v + d) % NZ)

    def chippeer(dy, dx):
        return (ybase[dy] + xbase[dx], v)

    def otherpeer(dy, dx):
        return (ybase[dy] + xbase[dx] + (1 - 2 * c), v)

    cpeer = (y * (NX * NC) + x * NC + 1 - c, v)

    barrier = pltpu.get_barrier_semaphore()

    def greet(peer):
        pl.semaphore_signal(barrier, inc=1, device_id=peer, device_id_type=MESH)

    for hops in range(NY // 2 + NX // 2, 0, -1):
        for dy, dx in CHIPOFF:
            if (dy == 0 or dx == 0) and ring(dy, NY) + ring(dx, NX) == hops:
                greet(chippeer(dy, dx))
                if dy == 0:
                    greet(otherpeer(dy, dx))
        for d in ZOFF:
            if ring(d, NZ) == hops:
                greet(zpeer(d))
    greet(cpeer)

    loads = [
        (order, ord_v), (beta, beta_v),
        (active.at[0:128], act_v.at[0:128]), (active.at[128:256], act_v.at[128:256]),
        (active.at[256:384], act_v.at[256:384]), (active.at[384:512], act_v.at[384:512]),
        (counts, cnt_v), (ipcw, ipcw_v), (events, ev_v), (screen, scr_v),
    ]
    loads = [pltpu.make_async_copy(a, b, load_sem.at[i]) for i, (a, b) in enumerate(loads)]
    for copy in loads:
        copy.start()

    def send(src, dst, ss, rs, peer):
        pltpu.make_async_remote_copy(
            src_ref=src, dst_ref=dst, send_sem=ss, recv_sem=rs, device_id=peer, device_id_type=MESH).start()

    def await_bytes(ref, sem):
        pltpu.make_async_copy(ref, ref, sem).wait()

    loads[1].wait()
    coefs = beta_v[...]
    for k in range(4):
        loads[2 + k].wait()
        part = lax.dot_general(
            coefs, act_v[k * 128:(k + 1) * 128, :], (((1,), (1,)), ((), ())), preferred_element_type=F32)
        h, lanes = k // 2, slice((k % 2) * 128, (k % 2) * 128 + 128)
        for dest in range(NZ):
            eta_send[dest, 4 * h:4 * h + 4, lanes] = part[4 * dest:4 * dest + 4, :]
    pl.semaphore_wait(barrier, NZ - 1 + NY - 1 + NX * NC - 1)
    for d in ZOFF:
        send(eta_send.at[(v + d) % NZ], eta_recv.at[d - 1], eta_ss, eta_rs, zpeer(d))

    for d in YOFF[:NY - 1]:
        pl.semaphore_signal(ready, inc=1, device_id=chippeer(d, 0), device_id_type=MESH)

    loads[0].wait()
    ranks = ord_v[...].astype(F32)
    for k in range(4):
        column = jnp.broadcast_to(ranks[:, k * 128:(k + 1) * 128], (128, 128)).T
        for j in range(4):
            line = jnp.broadcast_to(ranks[:, j * 128:(j + 1) * 128], (128, 128))
            later[k * 128:(k + 1) * 128, j * 128:(j + 1) * 128] = jnp.where(column >= line, 1.0, 0.0).astype(BF16)
            earlier[k * 128:(k + 1) * 128, j * 128:(j + 1) * 128] = jnp.where(column <= line, 1.0, 0.0).astype(BF16)
    for i in (6, 7, 8):
        loads[i].wait()
    wts = cnt_v[...].astype(F32) * ipcw_v[...]
    flagged = ev_v[...].astype(F32) * wts

    await_bytes(eta_recv, eta_rs)
    eta = eta_send[v]
    for d in range(1, NZ):
        eta = eta + eta_recv[d - 1]
    sum_send[...] = eta
    for d in ZOFF:
        send(sum_send, eta_all.at[v], all_ss, all_rs, zpeer(d))
    eta_all[v] = eta
    await_bytes(eta_all.at[0:NZ - 1], all_rs)
    top = row_iota((8, HALF)) < 4
    lows, highs = [], []
    for u in range(4):
        one, two = eta_all[2 * u], eta_all[2 * u + 1]
        lows.append(jnp.where(top, one, swap4(two)))
        highs.append(jnp.where(top, swap4(one), two))
    eta = jnp.concatenate([jnp.concatenate(lows, axis=0), jnp.concatenate(highs, axis=0)], axis=1)
    risk = wts * jnp.exp(eta)

    def pair_start(total):
        tot_own[...] = total
        send(tot_own, tot_peer, pair_ss, pair_rs, cpeer)

    def pair_end(total):
        await_bytes(tot_peer, pair_rs)
        peer = tot_peer[...]
        tot_chip[...] = total + peer
        return peer

    def chip_send(offsets):
        for dy, dx in offsets:
            send(tot_chip, tot_recv.at[chip], chip_ss, chip_rs, chippeer(dy, dx))

    def chip_end(wanted):
        await_bytes(tot_recv.at[0:CHIPS - 1], chip_rs)
        out = jnp.zeros((1, 128), F32)
        for k in range(CHIPS):
            out = out + jnp.where(wanted(k), tot_recv[k], 0.0)
        return out

    lane = lane_iota((8, 128))
    first32 = (lane // 32) % 2 == 0
    first64 = lane < 64

    def project(pieces, j, out):
        place = pl.multiple_of(((y + YOFF[j]) % NY) * HALF, HALF)
        for a, geno in enumerate((act_v, scr_v)):
            block = jnp.dot(pieces, geno[:, pl.ds(place, HALF)], preferred_element_type=F32)
            block = block[:BOOT] + block[BOOT:]
            for t in range(2):
                for p in range(2):
                    one = block[16 * p:16 * p + 8, t * 128:(t + 1) * 128]
                    two = block[16 * p + 8:16 * p + 16, t * 128:(t + 1) * 128]
                    out[0, j, a * 4 + t * 2 + p] = jnp.where(first32, one, pltpu.roll(two, 32, 1))
                    out[1, j, a * 4 + t * 2 + p] = jnp.where(first32, pltpu.roll(one, 96, 1), two)

    def spread(mine, theirs, j, out):
        for a in range(2):
            for t in range(2):
                i = a * 4 + t * 2
                one = mine[c, j, i] + theirs[j, i]
                two = mine[c, j, i + 1] + theirs[j, i + 1]
                out[2 * t, j, a] = jnp.where(first64, one, pltpu.roll(two, 64, 1))
                out[2 * t + 1, j, a] = jnp.where(first64, pltpu.roll(one, 64, 1), two)

    total = to_lanes(jnp.sum(risk, axis=1, keepdims=True))
    pl.semaphore_wait(ready, NY - 1)
    risk_own[...] = total
    for dy, dx in CHIPOFF:
        for peer in (chippeer(dy, dx), otherpeer(dy, dx)):
            send(risk_own, risk_all.at[s], risk_ss, risk_rs, peer)
    send(risk_own, risk_all.at[s], risk_ss, risk_rs, cpeer)
    pieces = split2(risk)
    suffix = jnp.dot(pieces, later[...], preferred_element_type=F32)
    suffix = suffix[:BOOT] + suffix[BOOT:]
    loads[9].wait()
    for j in range(NY):
        project(pieces, j, two_send)
    send(two_send.at[1 - c], two_recv, two_ss, two_rs, cpeer)
    await_bytes(two_recv, two_rs)
    for j in range(NY):
        spread(two_send, two_recv, j, far_send)
    for d in XOFF:
        send(far_send.at[(x + d) % NX], far_recv.at[d - 1], far_ss, far_rs, chippeer(0, d))

    await_bytes(risk_all.at[0:2 * CHIPS - 1], risk_rs)
    after = jnp.zeros((1, 128), F32)
    for k in range(2 * CHIPS):
        after = after + jnp.where(k > s, risk_all[k], 0.0)
    haz = flagged / (suffix + to_rows(after))

    total = to_lanes(jnp.sum(haz, axis=1, keepdims=True))
    pair_start(total)
    prefix = jnp.dot(split2(haz), earlier[...], preferred_element_type=F32)
    prefix = prefix[:BOOT] + prefix[BOOT:]
    peer = pair_end(total)
    prefix = prefix + to_rows(jnp.where(c == 1, peer, 0.0))
    pieces = split2(flagged - risk * prefix)

    size = NY // PARTS

    def to_x(j):
        await_bytes(core_recv.at[j], core_rs.at[j])
        spread(core_send, core_recv, j, x_send)
        if (j + 1) % size == 0:
            part = j // size
            piece = pl.ds(part * size, size)
            for d in XOFF:
                send(x_send.at[(x + d) % NX, piece], x_recv.at[part, d - 1], x_ss, x_rs.at[part], chippeer(0, d))

    for j in range(NY):
        project(pieces, j, core_send)
        send(core_send.at[1 - c, j], core_recv.at[j], core_ss.at[j], core_rs.at[j], cpeer)
        chip_send(CHIPOFF[4 * j:4 * j + 4])
        if j >= LAG:
            to_x(j - LAG)
    for j in range(NY - LAG, NY):
        to_x(j)

    line = chip_end(lambda k: k < NX * y)
    ahead = []
    for k in range(NX):
        ahead.append(line)
        line = line + jnp.where(x == k, tot_chip[...], tot_recv[NX * y + k])
    factors = []
    for d in range(NX):
        at = (x - d + NX) % NX
        line = ahead[0]
        for k in range(1, NX):
            line = jnp.where(at == k, ahead[k], line)
        rows = jnp.broadcast_to(to_rows(line), (BOOT, 128))
        tile = rows[0:8]
        for q in range(1, 4):
            tile = jnp.where(lane // 32 == q, rows[8 * q:8 * q + 8], tile)
        factors.append(tile)
    await_bytes(far_recv, far_rs)
    for part in range(PARTS):
        await_bytes(x_recv.at[part], x_rs.at[part])
        for j in range(part * size, (part + 1) * size):
            i = j - part * size
            less = factors[0] * far_send[x, j] + factors[1] * far_recv[0, j]
            less = less + (factors[2] * far_recv[1, j] + factors[3] * far_recv[2, j])
            full = (x_send[x, j] + x_recv[part, 0, i]) + (x_recv[part, 1, i] + x_recv[part, 2, i])
            y_send[j] = full - less
            if YOFF[j]:
                send(y_send.at[j], y_recv.at[j], y_ss, y_rs, chippeer(YOFF[j], 0))
    await_bytes(eta_recv, eta_ss)
    await_bytes(eta_all.at[0:NZ - 1], all_ss)
    await_bytes(risk_all.at[0:2 * CHIPS - 1], risk_ss)
    await_bytes(tot_peer, pair_ss)
    await_bytes(tot_recv.at[0:CHIPS - 1], chip_ss)
    await_bytes(two_recv, two_ss)
    for j in range(NY):
        await_bytes(core_recv.at[j], core_ss.at[j])
    await_bytes(x_recv, x_ss)
    await_bytes(far_recv, far_ss)
    await_bytes(y_recv, y_rs)
    final = y_send[NY - 1]
    for j in range(NY - 1):
        final = final + y_recv[j]
    final = final * scale
    for a in range(2):
        for q in range(4):
            turned = final[a] if q == 0 else pltpu.roll(final[a], 128 - 32 * q, 1)
            result[a, 8 * q:8 * q + 8, :] = turned[:, :32]
    await_bytes(y_recv, y_ss)


def per_device(active_geno, screen_geno, beta, counts, ipcw, events, order):
    rows, columns = active_geno.shape
    scale = float(rows * lax.axis_size("samp")) ** (-0.5)
    out = jax.ShapeDtypeStruct((2, BOOT, 32), F32)
    dma = pltpu.SemaphoreType.DMA
    result = pl.pallas_call(
        functools.partial(kernel, scale),
        out_shape=out,
        in_specs=[pl.BlockSpec(memory_space=pltpu.HBM)] * 7,
        out_specs=pl.BlockSpec(memory_space=pltpu.VMEM),
        scratch_shapes=[
            pltpu.VMEM((rows, columns), BF16), pltpu.VMEM((rows, columns), BF16),
            pltpu.VMEM((32, columns), BF16), pltpu.VMEM((32, rows), jnp.int32),
            pltpu.VMEM((1, rows), F32), pltpu.VMEM((1, rows), jnp.int32), pltpu.VMEM((1, rows), jnp.int32),
            pltpu.VMEM((rows, rows), BF16), pltpu.VMEM((rows, rows), BF16),
            pltpu.VMEM((NZ, 8, HALF), F32), pltpu.VMEM((NZ - 1, 8, HALF), F32),
            pltpu.VMEM((8, HALF), F32), pltpu.VMEM((NZ, 8, HALF), F32),
            pltpu.VMEM((1, 128), F32), pltpu.VMEM((2 * CHIPS, 1, 128), F32),
            pltpu.VMEM((1, 128), F32), pltpu.VMEM((1, 128), F32),
            pltpu.VMEM((1, 128), F32), pltpu.VMEM((CHIPS, 1, 128), F32),
            pltpu.VMEM((2, NY, 8, 8, 128), F32), pltpu.VMEM((NY, 8, 8, 128), F32),
            pltpu.VMEM((2, NY, 8, 8, 128), F32), pltpu.VMEM((NY, 8, 8, 128), F32),
            pltpu.VMEM((NX, NY, 2, 8, 128), F32), pltpu.VMEM((NX - 1, NY, 2, 8, 128), F32),
            pltpu.VMEM((NX, NY, 2, 8, 128), F32), pltpu.VMEM((PARTS, NX - 1, NY // PARTS, 2, 8, 128), F32),
            pltpu.VMEM((NY, 2, 8, 128), F32), pltpu.VMEM((NY - 1, 2, 8, 128), F32),
            dma((10,)), dma, dma, dma, dma, dma, dma, dma, dma, dma, dma,
            dma, dma, dma((NY,)), dma((NY,)), dma, dma, dma, dma((PARTS,)), dma, dma, pltpu.SemaphoreType.REGULAR,
        ],
        compiler_params=pltpu.CompilerParams(
            collective_id=0, has_side_effects=True, vmem_limit_bytes=60 * 1024 * 1024),
    )(active_geno, screen_geno, beta.T, counts, ipcw.reshape(1, -1), events.reshape(1, -1), order)
    return result[0], result[1]


def solution(mesh):
    placed = (
        P("samp", "var"),
        P("samp", "var"),
        P("var", None),
        P(None, "samp"),
        P("samp"),
        P("samp"),
        P("samp", None),
    )
    return jax.shard_map(
        per_device,
        mesh=mesh,
        in_specs=placed,
        out_specs=(P(None, ("var", "samp")), P(None, ("var", "samp"))),
        check_vma=False,
    )
```

```python
import functools
import jax
import jax.numpy as jnp
from jax import lax
from jax.experimental import pallas as pl
from jax.experimental.pallas import tpu as pltpu
from jax.sharding import PartitionSpec as P

MESH = pl.DeviceIdType.MESH
NY, NX, NC, NZ = 8, 4, 2, 8
CHIPS = NY * NX
BOOT = 32
HALF = 256
PARTS = 4
LAG = 3
F32 = jnp.float32
BF16 = jnp.bfloat16


def ring(d, n):
    return min(d, n - d)


ZOFF = sorted(range(1, NZ), key=lambda d: -ring(d, NZ))
YOFF = sorted(range(NY), key=lambda d: -ring(d, NY))
XOFF = sorted(range(1, NX), key=lambda d: -ring(d, NX))
CHIPOFF = sorted(
    [(dy, dx) for dy in range(NY) for dx in range(NX) if dy or dx],
    key=lambda o: -(ring(o[0], NY) + ring(o[1], NX)))


def lane_iota(shape):
    return lax.broadcasted_iota(jnp.int32, shape, 1)


def row_iota(shape):
    return lax.broadcasted_iota(jnp.int32, shape, 0)


def swap4(tile):
    return pltpu.roll(tile, 4, 0)


def split2(value):
    high = value.astype(BF16)
    rest = (value - high.astype(F32)).astype(BF16)
    return jnp.concatenate([high, rest], axis=0)


def to_lanes(total):
    full = jnp.broadcast_to(total, (BOOT, 128))
    same = lane_iota((BOOT, 128)) == row_iota((BOOT, 128))
    return jnp.sum(jnp.where(same, full, 0.0), axis=0, keepdims=True)


def to_rows(line):
    full = jnp.broadcast_to(line, (BOOT, 128))
    same = lane_iota((BOOT, 128)) == row_iota((BOOT, 128))
    return jnp.sum(jnp.where(same, full, 0.0), axis=1, keepdims=True)


def kernel(scale, active, screen, beta, counts, ipcw, events, order, result,
           act_v, scr_v, beta_v, cnt_v, ipcw_v, ev_v, ord_v,
           later, earlier, eta_send, eta_recv, sum_send, eta_all,
           risk_own, risk_all, tot_own, tot_peer, tot_chip, tot_recv,
           two_send, two_recv, core_send, core_recv, far_send, far_recv, x_send, x_recv, y_send, y_recv,
           load_sem, eta_ss, eta_rs, all_ss, all_rs, risk_ss, risk_rs, pair_ss, pair_rs, chip_ss, chip_rs,
           two_ss, two_rs, core_ss, core_rs, far_ss, far_rs, x_ss, x_rs, y_ss, y_rs, ready):
    s = lax.axis_index("samp")
    v = lax.axis_index("var")
    y, g = s // (NX * NC), s % (NX * NC)
    x, c = g // NC, g % NC
    ybase = [((y + d) % NY) * (NX * NC) for d in range(NY)]
    xbase = [((x + d) % NX) * NC + c for d in range(NX)]
    chip = y * NX + x

    def zpeer(d):
        return (s, (v + d) % NZ)

    def chippeer(dy, dx):
        return (ybase[dy] + xbase[dx], v)

    def otherpeer(dy, dx):
        return (ybase[dy] + xbase[dx] + (1 - 2 * c), v)

    cpeer = (y * (NX * NC) + x * NC + 1 - c, v)

    barrier = pltpu.get_barrier_semaphore()

    def greet(peer):
        pl.semaphore_signal(barrier, inc=1, device_id=peer, device_id_type=MESH)

    for hops in range(NY // 2 + NX // 2, 0, -1):
        for dy, dx in CHIPOFF:
            if (dy == 0 or dx == 0) and ring(dy, NY) + ring(dx, NX) == hops:
                greet(chippeer(dy, dx))
                if dy == 0:
                    greet(otherpeer(dy, dx))
        for d in ZOFF:
            if ring(d, NZ) == hops:
                greet(zpeer(d))
    greet(cpeer)

    loads = [
        (order, ord_v), (beta, beta_v),
        (active.at[0:128], act_v.at[0:128]), (active.at[128:256], act_v.at[128:256]),
        (active.at[256:384], act_v.at[256:384]), (active.at[384:512], act_v.at[384:512]),
        (counts, cnt_v), (ipcw, ipcw_v), (events, ev_v), (screen, scr_v),
    ]
    loads = [pltpu.make_async_copy(a, b, load_sem.at[i]) for i, (a, b) in enumerate(loads)]
    for copy in loads:
        copy.start()

    def send(src, dst, ss, rs, peer):
        pltpu.make_async_remote_copy(
            src_ref=src, dst_ref=dst, send_sem=ss, recv_sem=rs, device_id=peer, device_id_type=MESH).start()

    def await_bytes(ref, sem):
        pltpu.make_async_copy(ref, ref, sem).wait()

    loads[1].wait()
    coefs = beta_v[...]
    for k in range(4):
        loads[2 + k].wait()
        part = lax.dot_general(
            coefs, act_v[k * 128:(k + 1) * 128, :], (((1,), (1,)), ((), ())), preferred_element_type=F32)
        h, lanes = k // 2, slice((k % 2) * 128, (k % 2) * 128 + 128)
        for dest in range(NZ):
            eta_send[dest, 4 * h:4 * h + 4, lanes] = part[4 * dest:4 * dest + 4, :]
    pl.semaphore_wait(barrier, NZ - 1 + NY - 1 + NX * NC - 1)
    for d in ZOFF:
        send(eta_send.at[(v + d) % NZ], eta_recv.at[d - 1], eta_ss, eta_rs, zpeer(d))

    for d in YOFF[:NY - 1]:
        pl.semaphore_signal(ready, inc=1, device_id=chippeer(d, 0), device_id_type=MESH)

    loads[0].wait()
    ranks = ord_v[...].astype(F32)
    for k in range(4):
        column = jnp.broadcast_to(ranks[:, k * 128:(k + 1) * 128], (128, 128)).T
        for j in range(4):
            line = jnp.broadcast_to(ranks[:, j * 128:(j + 1) * 128], (128, 128))
            later[k * 128:(k + 1) * 128, j * 128:(j + 1) * 128] = jnp.where(column >= line, 1.0, 0.0).astype(BF16)
            earlier[k * 128:(k + 1) * 128, j * 128:(j + 1) * 128] = jnp.where(column <= line, 1.0, 0.0).astype(BF16)
    for i in (6, 7, 8):
        loads[i].wait()
    wts = cnt_v[...].astype(F32) * ipcw_v[...]
    flagged = ev_v[...].astype(F32) * wts

    await_bytes(eta_recv, eta_rs)
    eta = eta_send[v]
    for d in range(1, NZ):
        eta = eta + eta_recv[d - 1]
    sum_send[...] = eta
    for d in ZOFF:
        send(sum_send, eta_all.at[v], all_ss, all_rs, zpeer(d))
    eta_all[v] = eta
    await_bytes(eta_all.at[0:NZ - 1], all_rs)
    top = row_iota((8, HALF)) < 4
    lows, highs = [], []
    for u in range(4):
        one, two = eta_all[2 * u], eta_all[2 * u + 1]
        lows.append(jnp.where(top, one, swap4(two)))
        highs.append(jnp.where(top, swap4(one), two))
    eta = jnp.concatenate([jnp.concatenate(lows, axis=0), jnp.concatenate(highs, axis=0)], axis=1)
    risk = wts * jnp.exp(eta)

    def pair_start(total):
        tot_own[...] = total
        send(tot_own, tot_peer, pair_ss, pair_rs, cpeer)

    def pair_end(total):
        await_bytes(tot_peer, pair_rs)
        peer = tot_peer[...]
        tot_chip[...] = total + peer
        return peer

    def chip_send(offsets):
        for dy, dx in offsets:
            send(tot_chip, tot_recv.at[chip], chip_ss, chip_rs, chippeer(dy, dx))

    def chip_end(wanted):
        await_bytes(tot_recv.at[0:CHIPS - 1], chip_rs)
        out = jnp.zeros((1, 128), F32)
        for k in range(CHIPS):
            out = out + jnp.where(wanted(k), tot_recv[k], 0.0)
        return out

    lane = lane_iota((8, 128))
    first32 = (lane // 32) % 2 == 0
    first64 = lane < 64

    def project(pieces, j, out):
        place = pl.multiple_of(((y + YOFF[j]) % NY) * HALF, HALF)
        for a, geno in enumerate((act_v, scr_v)):
            block = jnp.dot(pieces, geno[:, pl.ds(place, HALF)], preferred_element_type=F32)
            block = block[:BOOT] + block[BOOT:]
            for t in range(2):
                for p in range(2):
                    one = block[16 * p:16 * p + 8, t * 128:(t + 1) * 128]
                    two = block[16 * p + 8:16 * p + 16, t * 128:(t + 1) * 128]
                    out[0, j, a * 4 + t * 2 + p] = jnp.where(first32, one, pltpu.roll(two, 32, 1))
                    out[1, j, a * 4 + t * 2 + p] = jnp.where(first32, pltpu.roll(one, 96, 1), two)

    def spread(mine, theirs, j, out):
        for a in range(2):
            for t in range(2):
                i = a * 4 + t * 2
                one = mine[c, j, i] + theirs[j, i]
                two = mine[c, j, i + 1] + theirs[j, i + 1]
                out[2 * t, j, a] = jnp.where(first64, one, pltpu.roll(two, 64, 1))
                out[2 * t + 1, j, a] = jnp.where(first64, pltpu.roll(one, 64, 1), two)

    total = to_lanes(jnp.sum(risk, axis=1, keepdims=True))
    pl.semaphore_wait(ready, NY - 1)
    risk_own[...] = total
    for dy, dx in CHIPOFF:
        for peer in (chippeer(dy, dx), otherpeer(dy, dx)):
            send(risk_own, risk_all.at[s], risk_ss, risk_rs, peer)
    send(risk_own, risk_all.at[s], risk_ss, risk_rs, cpeer)
    pieces = split2(risk)
    suffix = jnp.dot(pieces, later[...], preferred_element_type=F32)
    suffix = suffix[:BOOT] + suffix[BOOT:]
    loads[9].wait()
    for j in range(NY):
        project(pieces, j, two_send)
    send(two_send.at[1 - c], two_recv, two_ss, two_rs, cpeer)
    await_bytes(two_recv, two_rs)
    for j in range(NY):
        spread(two_send, two_recv, j, far_send)
    for d in XOFF:
        send(far_send.at[(x + d) % NX], far_recv.at[d - 1], far_ss, far_rs, chippeer(0, d))

    await_bytes(risk_all.at[0:2 * CHIPS - 1], risk_rs)
    after = jnp.zeros((1, 128), F32)
    for k in range(2 * CHIPS):
        after = after + jnp.where(k > s, risk_all[k], 0.0)
    haz = flagged / (suffix + to_rows(after))

    total = to_lanes(jnp.sum(haz, axis=1, keepdims=True))
    pair_start(total)
    prefix = jnp.dot(split2(haz), earlier[...], preferred_element_type=F32)
    prefix = prefix[:BOOT] + prefix[BOOT:]
    pieces = split2(flagged - risk * prefix)

    size = NY // PARTS

    def to_x(j, factors):
        await_bytes(core_recv.at[j], core_rs.at[j])
        for i in range(8):
            less = factors[0][i % 2] * two_send[c, j, i] + factors[1][i % 2] * two_recv[j, i]
            core_recv[j, i] = core_recv[j, i] - less
        spread(core_send, core_recv, j, x_send)
        if (j + 1) % size == 0:
            part = j // size
            piece = pl.ds(part * size, size)
            for d in XOFF:
                send(x_send.at[(x + d) % NX, piece], x_recv.at[part, d - 1], x_ss, x_rs.at[part], chippeer(0, d))

    def by_core(line):
        rows = jnp.broadcast_to(to_rows(line), (BOOT, 128))
        return [jnp.where(first32, rows[16 * p:16 * p + 8], rows[16 * p + 8:16 * p + 16]) for p in range(2)]

    factors = None
    for j in range(NY):
        project(pieces, j, core_send)
        send(core_send.at[1 - c, j], core_recv.at[j], core_ss.at[j], core_rs.at[j], cpeer)
        if j == 1:
            peer = pair_end(total)
            factors = by_core(jnp.where(c == 1, peer, 0.0)), by_core(jnp.where(c == 0, total, 0.0))
        if j >= 1:
            chip_send(CHIPOFF[5 * (j - 1):5 * j])
        if j >= LAG:
            to_x(j - LAG, factors)
    for j in range(NY - LAG, NY):
        to_x(j, factors)

    line = chip_end(lambda k: k < NX * y)
    ahead = []
    for k in range(NX):
        ahead.append(line)
        line = line + jnp.where(x == k, tot_chip[...], tot_recv[NX * y + k])
    factors = []
    for d in range(NX):
        at = (x - d + NX) % NX
        line = ahead[0]
        for k in range(1, NX):
            line = jnp.where(at == k, ahead[k], line)
        rows = jnp.broadcast_to(to_rows(line), (BOOT, 128))
        tile = rows[0:8]
        for q in range(1, 4):
            tile = jnp.where(lane // 32 == q, rows[8 * q:8 * q + 8], tile)
        factors.append(tile)
    await_bytes(far_recv, far_rs)
    for part in range(PARTS):
        await_bytes(x_recv.at[part], x_rs.at[part])
        for j in range(part * size, (part + 1) * size):
            i = j - part * size
            less = factors[0] * far_send[x, j] + factors[1] * far_recv[0, j]
            less = less + (factors[2] * far_recv[1, j] + factors[3] * far_recv[2, j])
            full = (x_send[x, j] + x_recv[part, 0, i]) + (x_recv[part, 1, i] + x_recv[part, 2, i])
            y_send[j] = full - less
            if YOFF[j]:
                send(y_send.at[j], y_recv.at[j], y_ss, y_rs, chippeer(YOFF[j], 0))
    await_bytes(eta_recv, eta_ss)
    await_bytes(eta_all.at[0:NZ - 1], all_ss)
    await_bytes(risk_all.at[0:2 * CHIPS - 1], risk_ss)
    await_bytes(tot_peer, pair_ss)
    await_bytes(tot_recv.at[0:CHIPS - 1], chip_ss)
    await_bytes(two_recv, two_ss)
    for j in range(NY):
        await_bytes(core_recv.at[j], core_ss.at[j])
    await_bytes(x_recv, x_ss)
    await_bytes(far_recv, far_ss)
    await_bytes(y_recv, y_rs)
    final = y_send[NY - 1]
    for j in range(NY - 1):
        final = final + y_recv[j]
    final = final * scale
    for a in range(2):
        for q in range(4):
            turned = final[a] if q == 0 else pltpu.roll(final[a], 128 - 32 * q, 1)
            result[a, 8 * q:8 * q + 8, :] = turned[:, :32]
    await_bytes(y_recv, y_ss)


def per_device(active_geno, screen_geno, beta, counts, ipcw, events, order):
    rows, columns = active_geno.shape
    scale = float(rows * lax.axis_size("samp")) ** (-0.5)
    out = jax.ShapeDtypeStruct((2, BOOT, 32), F32)
    dma = pltpu.SemaphoreType.DMA
    result = pl.pallas_call(
        functools.partial(kernel, scale),
        out_shape=out,
        in_specs=[pl.BlockSpec(memory_space=pltpu.HBM)] * 7,
        out_specs=pl.BlockSpec(memory_space=pltpu.VMEM),
        scratch_shapes=[
            pltpu.VMEM((rows, columns), BF16), pltpu.VMEM((rows, columns), BF16),
            pltpu.VMEM((32, columns), BF16), pltpu.VMEM((32, rows), jnp.int32),
            pltpu.VMEM((1, rows), F32), pltpu.VMEM((1, rows), jnp.int32), pltpu.VMEM((1, rows), jnp.int32),
            pltpu.VMEM((rows, rows), BF16), pltpu.VMEM((rows, rows), BF16),
            pltpu.VMEM((NZ, 8, HALF), F32), pltpu.VMEM((NZ - 1, 8, HALF), F32),
            pltpu.VMEM((8, HALF), F32), pltpu.VMEM((NZ, 8, HALF), F32),
            pltpu.VMEM((1, 128), F32), pltpu.VMEM((2 * CHIPS, 1, 128), F32),
            pltpu.VMEM((1, 128), F32), pltpu.VMEM((1, 128), F32),
            pltpu.VMEM((1, 128), F32), pltpu.VMEM((CHIPS, 1, 128), F32),
            pltpu.VMEM((2, NY, 8, 8, 128), F32), pltpu.VMEM((NY, 8, 8, 128), F32),
            pltpu.VMEM((2, NY, 8, 8, 128), F32), pltpu.VMEM((NY, 8, 8, 128), F32),
            pltpu.VMEM((NX, NY, 2, 8, 128), F32), pltpu.VMEM((NX - 1, NY, 2, 8, 128), F32),
            pltpu.VMEM((NX, NY, 2, 8, 128), F32), pltpu.VMEM((PARTS, NX - 1, NY // PARTS, 2, 8, 128), F32),
            pltpu.VMEM((NY, 2, 8, 128), F32), pltpu.VMEM((NY - 1, 2, 8, 128), F32),
            dma((10,)), dma, dma, dma, dma, dma, dma, dma, dma, dma, dma,
            dma, dma, dma((NY,)), dma((NY,)), dma, dma, dma, dma((PARTS,)), dma, dma, pltpu.SemaphoreType.REGULAR,
        ],
        compiler_params=pltpu.CompilerParams(
            collective_id=0, has_side_effects=True, vmem_limit_bytes=60 * 1024 * 1024),
    )(active_geno, screen_geno, beta.T, counts, ipcw.reshape(1, -1), events.reshape(1, -1), order)
    return result[0], result[1]


def solution(mesh):
    placed = (
        P("samp", "var"),
        P("samp", "var"),
        P("var", None),
        P(None, "samp"),
        P("samp"),
        P("samp"),
        P("samp", None),
    )
    return jax.shard_map(
        per_device,
        mesh=mesh,
        in_specs=placed,
        out_specs=(P(None, ("var", "samp")), P(None, ("var", "samp"))),
        check_vma=False,
    )
```

```python
import functools
import jax
import jax.numpy as jnp
from jax import lax
from jax.experimental import pallas as pl
from jax.experimental.pallas import tpu as pltpu
from jax.sharding import PartitionSpec as P

MESH = pl.DeviceIdType.MESH
NY, NX, NC, NZ = 8, 4, 2, 8
CHIPS = NY * NX
BOOT = 32
HALF = 256
PARTS = 4
LAG = 3
F32 = jnp.float32
BF16 = jnp.bfloat16


def ring(d, n):
    return min(d, n - d)


ZOFF = sorted(range(1, NZ), key=lambda d: -ring(d, NZ))
YOFF = sorted(range(NY), key=lambda d: -ring(d, NY))
XOFF = sorted(range(1, NX), key=lambda d: -ring(d, NX))
CHIPOFF = sorted(
    [(dy, dx) for dy in range(NY) for dx in range(NX) if dy or dx],
    key=lambda o: -(ring(o[0], NY) + ring(o[1], NX)))


def lane_iota(shape):
    return lax.broadcasted_iota(jnp.int32, shape, 1)


def row_iota(shape):
    return lax.broadcasted_iota(jnp.int32, shape, 0)


def swap4(tile):
    return pltpu.roll(tile, 4, 0)


def split2(value):
    high = value.astype(BF16)
    rest = (value - high.astype(F32)).astype(BF16)
    return jnp.concatenate([high, rest], axis=0)


def to_lanes(total):
    full = jnp.broadcast_to(total, (BOOT, 128))
    same = lane_iota((BOOT, 128)) == row_iota((BOOT, 128))
    return jnp.sum(jnp.where(same, full, 0.0), axis=0, keepdims=True)


def to_rows(line):
    full = jnp.broadcast_to(line, (BOOT, 128))
    same = lane_iota((BOOT, 128)) == row_iota((BOOT, 128))
    return jnp.sum(jnp.where(same, full, 0.0), axis=1, keepdims=True)


def kernel(scale, active, screen, beta, counts, ipcw, events, order, result,
           act_v, scr_v, beta_v, cnt_v, ipcw_v, ev_v, ord_v,
           later, earlier, eta_send, eta_recv, sum_send, eta_all,
           risk_own, risk_all, tot_own, tot_peer, tot_chip, tot_recv,
           two_send, two_recv, core_send, core_recv, far_send, far_recv, x_send, x_recv, y_send, y_recv,
           load_sem, eta_ss, eta_rs, all_ss, all_rs, risk_ss, risk_rs, pair_ss, pair_rs, chip_ss, chip_rs,
           two_ss, two_rs, core_ss, core_rs, far_ss, far_rs, x_ss, x_rs, y_ss, y_rs, ready):
    s = lax.axis_index("samp")
    v = lax.axis_index("var")
    y, g = s // (NX * NC), s % (NX * NC)
    x, c = g // NC, g % NC
    ybase = [((y + d) % NY) * (NX * NC) for d in range(NY)]
    xbase = [((x + d) % NX) * NC + c for d in range(NX)]
    chip = y * NX + x

    def zpeer(d):
        return (s, (v + d) % NZ)

    def chippeer(dy, dx):
        return (ybase[dy] + xbase[dx], v)

    def otherpeer(dy, dx):
        return (ybase[dy] + xbase[dx] + (1 - 2 * c), v)

    cpeer = (y * (NX * NC) + x * NC + 1 - c, v)

    barrier = pltpu.get_barrier_semaphore()

    def greet(peer):
        pl.semaphore_signal(barrier, inc=1, device_id=peer, device_id_type=MESH)

    for hops in range(NY // 2 + NX // 2, 0, -1):
        for dy, dx in CHIPOFF:
            if (dy == 0 or dx == 0) and ring(dy, NY) + ring(dx, NX) == hops:
                greet(chippeer(dy, dx))
                if dy == 0:
                    greet(otherpeer(dy, dx))
        for d in ZOFF:
            if ring(d, NZ) == hops:
                greet(zpeer(d))
    greet(cpeer)

    loads = [
        (order, ord_v), (beta, beta_v),
        (active.at[0:128], act_v.at[0:128]), (active.at[128:256], act_v.at[128:256]),
        (active.at[256:384], act_v.at[256:384]), (active.at[384:512], act_v.at[384:512]),
        (counts, cnt_v), (ipcw, ipcw_v), (events, ev_v), (screen, scr_v),
    ]
    loads = [pltpu.make_async_copy(a, b, load_sem.at[i]) for i, (a, b) in enumerate(loads)]
    for copy in loads:
        copy.start()

    def send(src, dst, ss, rs, peer):
        pltpu.make_async_remote_copy(
            src_ref=src, dst_ref=dst, send_sem=ss, recv_sem=rs, device_id=peer, device_id_type=MESH).start()

    def await_bytes(ref, sem):
        pltpu.make_async_copy(ref, ref, sem).wait()

    loads[1].wait()
    coefs = beta_v[...]
    for k in range(4):
        loads[2 + k].wait()
        part = lax.dot_general(
            coefs, act_v[k * 128:(k + 1) * 128, :], (((1,), (1,)), ((), ())), preferred_element_type=F32)
        h, lanes = k // 2, slice((k % 2) * 128, (k % 2) * 128 + 128)
        for dest in range(NZ):
            eta_send[dest, 4 * h:4 * h + 4, lanes] = part[4 * dest:4 * dest + 4, :]
    pl.semaphore_wait(barrier, NZ - 1 + NY - 1 + NX * NC - 1)
    for d in ZOFF:
        send(eta_send.at[(v + d) % NZ], eta_recv.at[d - 1], eta_ss, eta_rs, zpeer(d))

    for d in YOFF[:NY - 1]:
        pl.semaphore_signal(ready, inc=1, device_id=chippeer(d, 0), device_id_type=MESH)

    loads[0].wait()
    ranks = ord_v[...].astype(F32)
    for k in range(4):
        column = jnp.broadcast_to(ranks[:, k * 128:(k + 1) * 128], (128, 128)).T
        for j in range(4):
            line = jnp.broadcast_to(ranks[:, j * 128:(j + 1) * 128], (128, 128))
            later[k * 128:(k + 1) * 128, j * 128:(j + 1) * 128] = jnp.where(column >= line, 1.0, 0.0).astype(BF16)
            earlier[k * 128:(k + 1) * 128, j * 128:(j + 1) * 128] = jnp.where(column <= line, 1.0, 0.0).astype(BF16)
    for i in (6, 7, 8):
        loads[i].wait()
    wts = cnt_v[...].astype(F32) * ipcw_v[...]
    flagged = ev_v[...].astype(F32) * wts

    await_bytes(eta_recv, eta_rs)
    eta = eta_send[v]
    for d in range(1, NZ):
        eta = eta + eta_recv[d - 1]
    sum_send[...] = eta
    for d in ZOFF:
        send(sum_send, eta_all.at[v], all_ss, all_rs, zpeer(d))
    eta_all[v] = eta
    await_bytes(eta_all.at[0:NZ - 1], all_rs)
    top = row_iota((8, HALF)) < 4
    lows, highs = [], []
    for u in range(4):
        one, two = eta_all[2 * u], eta_all[2 * u + 1]
        lows.append(jnp.where(top, one, swap4(two)))
        highs.append(jnp.where(top, swap4(one), two))
    eta = jnp.concatenate([jnp.concatenate(lows, axis=0), jnp.concatenate(highs, axis=0)], axis=1)
    risk = wts * jnp.exp(eta)

    def pair_start(total):
        tot_own[...] = total
        send(tot_own, tot_peer, pair_ss, pair_rs, cpeer)

    def pair_end(total):
        await_bytes(tot_peer, pair_rs)
        peer = tot_peer[...]
        tot_chip[...] = total + peer
        return peer

    def chip_send(offsets):
        for dy, dx in offsets:
            send(tot_chip, tot_recv.at[chip], chip_ss, chip_rs, chippeer(dy, dx))

    def chip_end(wanted):
        await_bytes(tot_recv.at[0:CHIPS - 1], chip_rs)
        out = jnp.zeros((1, 128), F32)
        for k in range(CHIPS):
            out = out + jnp.where(wanted(k), tot_recv[k], 0.0)
        return out

    lane = lane_iota((8, 128))
    first32 = (lane // 32) % 2 == 0
    first64 = lane < 64

    def project(pieces, j, out):
        place = pl.multiple_of(((y + YOFF[j]) % NY) * HALF, HALF)
        for a, geno in enumerate((act_v, scr_v)):
            block = jnp.dot(pieces, geno[:, pl.ds(place, HALF)], preferred_element_type=F32)
            block = block[:BOOT] + block[BOOT:]
            for t in range(2):
                for p in range(2):
                    one = block[16 * p:16 * p + 8, t * 128:(t + 1) * 128]
                    two = block[16 * p + 8:16 * p + 16, t * 128:(t + 1) * 128]
                    out[0, j, a * 4 + t * 2 + p] = jnp.where(first32, one, pltpu.roll(two, 32, 1))
                    out[1, j, a * 4 + t * 2 + p] = jnp.where(first32, pltpu.roll(one, 96, 1), two)

    def spread(mine, theirs, j, out):
        for a in range(2):
            for t in range(2):
                i = a * 4 + t * 2
                one = mine[c, j, i] + theirs[j, i]
                two = mine[c, j, i + 1] + theirs[j, i + 1]
                out[2 * t, j, a] = jnp.where(first64, one, pltpu.roll(two, 64, 1))
                out[2 * t + 1, j, a] = jnp.where(first64, pltpu.roll(one, 64, 1), two)

    total = to_lanes(jnp.sum(risk, axis=1, keepdims=True))
    pl.semaphore_wait(ready, NY - 1)
    risk_own[...] = total
    for dy, dx in CHIPOFF:
        for peer in (chippeer(dy, dx), otherpeer(dy, dx)):
            send(risk_own, risk_all.at[s], risk_ss, risk_rs, peer)
    send(risk_own, risk_all.at[s], risk_ss, risk_rs, cpeer)
    pieces = split2(risk)
    suffix = jnp.dot(pieces, later[...], preferred_element_type=F32)
    suffix = suffix[:BOOT] + suffix[BOOT:]
    loads[9].wait()
    for j in range(NY):
        project(pieces, j, two_send)
    send(two_send.at[1 - c], two_recv, two_ss, two_rs, cpeer)
    await_bytes(two_recv, two_rs)
    for j in range(NY):
        spread(two_send, two_recv, j, far_send)
    for d in XOFF:
        send(far_send.at[(x + d) % NX], far_recv.at[d - 1], far_ss, far_rs, chippeer(0, d))

    await_bytes(risk_all.at[0:2 * CHIPS - 1], risk_rs)
    chains = [jnp.zeros((1, 128), F32) for _ in range(4)]
    for k in range(2 * CHIPS):
        chains[k % 4] = chains[k % 4] + jnp.where(k > s, risk_all[k], 0.0)
    after = (chains[0] + chains[1]) + (chains[2] + chains[3])
    haz = flagged / (suffix + to_rows(after))

    total = to_lanes(jnp.sum(haz, axis=1, keepdims=True))
    pair_start(total)
    prefix = jnp.dot(split2(haz), earlier[...], preferred_element_type=F32)
    prefix = prefix[:BOOT] + prefix[BOOT:]
    pieces = split2(flagged - risk * prefix)

    size = NY // PARTS

    def to_x(j, factors):
        await_bytes(core_recv.at[j], core_rs.at[j])
        for i in range(8):
            less = factors[0][i % 2] * two_send[c, j, i] + factors[1][i % 2] * two_recv[j, i]
            core_recv[j, i] = core_recv[j, i] - less
        spread(core_send, core_recv, j, x_send)
        if (j + 1) % size == 0:
            part = j // size
            piece = pl.ds(part * size, size)
            for d in XOFF:
                send(x_send.at[(x + d) % NX, piece], x_recv.at[part, d - 1], x_ss, x_rs.at[part], chippeer(0, d))

    def by_core(line):
        rows = jnp.broadcast_to(to_rows(line), (BOOT, 128))
        return [jnp.where(first32, rows[16 * p:16 * p + 8], rows[16 * p + 8:16 * p + 16]) for p in range(2)]

    factors = None
    for j in range(NY):
        project(pieces, j, core_send)
        send(core_send.at[1 - c, j], core_recv.at[j], core_ss.at[j], core_rs.at[j], cpeer)
        if j == 1:
            peer = pair_end(total)
            factors = by_core(jnp.where(c == 1, peer, 0.0)), by_core(jnp.where(c == 0, total, 0.0))
        if j >= 1:
            chip_send(CHIPOFF[5 * (j - 1):5 * j])
        if j >= LAG:
            to_x(j - LAG, factors)
    for j in range(NY - LAG, NY):
        to_x(j, factors)

    line = chip_end(lambda k: k < NX * y)
    ahead = []
    for k in range(NX):
        ahead.append(line)
        line = line + jnp.where(x == k, tot_chip[...], tot_recv[NX * y + k])
    factors = []
    for d in range(NX):
        at = (x - d + NX) % NX
        line = ahead[0]
        for k in range(1, NX):
            line = jnp.where(at == k, ahead[k], line)
        rows = jnp.broadcast_to(to_rows(line), (BOOT, 128))
        tile = rows[0:8]
        for q in range(1, 4):
            tile = jnp.where(lane // 32 == q, rows[8 * q:8 * q + 8], tile)
        factors.append(tile)
    await_bytes(far_recv, far_rs)
    for part in range(PARTS):
        await_bytes(x_recv.at[part], x_rs.at[part])
        for j in range(part * size, (part + 1) * size):
            i = j - part * size
            less = factors[0] * far_send[x, j] + factors[1] * far_recv[0, j]
            less = less + (factors[2] * far_recv[1, j] + factors[3] * far_recv[2, j])
            full = (x_send[x, j] + x_recv[part, 0, i]) + (x_recv[part, 1, i] + x_recv[part, 2, i])
            y_send[j] = full - less
            if YOFF[j]:
                send(y_send.at[j], y_recv.at[j], y_ss, y_rs, chippeer(YOFF[j], 0))
    await_bytes(eta_recv, eta_ss)
    await_bytes(eta_all.at[0:NZ - 1], all_ss)
    await_bytes(risk_all.at[0:2 * CHIPS - 1], risk_ss)
    await_bytes(tot_peer, pair_ss)
    await_bytes(tot_recv.at[0:CHIPS - 1], chip_ss)
    await_bytes(two_recv, two_ss)
    for j in range(NY):
        await_bytes(core_recv.at[j], core_ss.at[j])
    await_bytes(x_recv, x_ss)
    await_bytes(far_recv, far_ss)
    await_bytes(y_recv, y_rs)
    final = y_send[NY - 1]
    for j in range(NY - 1):
        final = final + y_recv[j]
    final = final * scale
    for a in range(2):
        for q in range(4):
            turned = final[a] if q == 0 else pltpu.roll(final[a], 128 - 32 * q, 1)
            result[a, 8 * q:8 * q + 8, :] = turned[:, :32]
    await_bytes(y_recv, y_ss)


def per_device(active_geno, screen_geno, beta, counts, ipcw, events, order):
    rows, columns = active_geno.shape
    scale = float(rows * lax.axis_size("samp")) ** (-0.5)
    out = jax.ShapeDtypeStruct((2, BOOT, 32), F32)
    dma = pltpu.SemaphoreType.DMA
    result = pl.pallas_call(
        functools.partial(kernel, scale),
        out_shape=out,
        in_specs=[pl.BlockSpec(memory_space=pltpu.HBM)] * 7,
        out_specs=pl.BlockSpec(memory_space=pltpu.VMEM),
        scratch_shapes=[
            pltpu.VMEM((rows, columns), BF16), pltpu.VMEM((rows, columns), BF16),
            pltpu.VMEM((32, columns), BF16), pltpu.VMEM((32, rows), jnp.int32),
            pltpu.VMEM((1, rows), F32), pltpu.VMEM((1, rows), jnp.int32), pltpu.VMEM((1, rows), jnp.int32),
            pltpu.VMEM((rows, rows), BF16), pltpu.VMEM((rows, rows), BF16),
            pltpu.VMEM((NZ, 8, HALF), F32), pltpu.VMEM((NZ - 1, 8, HALF), F32),
            pltpu.VMEM((8, HALF), F32), pltpu.VMEM((NZ, 8, HALF), F32),
            pltpu.VMEM((1, 128), F32), pltpu.VMEM((2 * CHIPS, 1, 128), F32),
            pltpu.VMEM((1, 128), F32), pltpu.VMEM((1, 128), F32),
            pltpu.VMEM((1, 128), F32), pltpu.VMEM((CHIPS, 1, 128), F32),
            pltpu.VMEM((2, NY, 8, 8, 128), F32), pltpu.VMEM((NY, 8, 8, 128), F32),
            pltpu.VMEM((2, NY, 8, 8, 128), F32), pltpu.VMEM((NY, 8, 8, 128), F32),
            pltpu.VMEM((NX, NY, 2, 8, 128), F32), pltpu.VMEM((NX - 1, NY, 2, 8, 128), F32),
            pltpu.VMEM((NX, NY, 2, 8, 128), F32), pltpu.VMEM((PARTS, NX - 1, NY // PARTS, 2, 8, 128), F32),
            pltpu.VMEM((NY, 2, 8, 128), F32), pltpu.VMEM((NY - 1, 2, 8, 128), F32),
            dma((10,)), dma, dma, dma, dma, dma, dma, dma, dma, dma, dma,
            dma, dma, dma((NY,)), dma((NY,)), dma, dma, dma, dma((PARTS,)), dma, dma, pltpu.SemaphoreType.REGULAR,
        ],
        compiler_params=pltpu.CompilerParams(
            collective_id=0, has_side_effects=True, vmem_limit_bytes=60 * 1024 * 1024),
    )(active_geno, screen_geno, beta.T, counts, ipcw.reshape(1, -1), events.reshape(1, -1), order)
    return result[0], result[1]


def solution(mesh):
    placed = (
        P("samp", "var"),
        P("samp", "var"),
        P("var", None),
        P(None, "samp"),
        P("samp"),
        P("samp"),
        P("samp", None),
    )
    return jax.shard_map(
        per_device,
        mesh=mesh,
        in_specs=placed,
        out_specs=(P(None, ("var", "samp")), P(None, ("var", "samp"))),
        check_vma=False,
    )
```
